32 devices in a mesh: dp: 4 (over z), seq: 8 (over y, x, core).
Axes of the slice: x: 2, y: 2, z: 4, core: 2. Of those that a mesh axis runs over, the one named last changes fastest.
Arguments:
- seq_in: bfloat16 [8192, 1536], P(('dp', 'seq')), parts along dimension 0, may hold values from -6 to 6
- conv_gain: float32 [1536], replicated, may hold values from 0.1 to 1.9
- convolution_weight: bfloat16 [3, 1536, 768], replicated, may hold values from -0.09375 to 0.09375
- conv_bias: float32 [768], replicated, may hold values from -3 to 3
- attn_gain: float32 [1536], replicated, may hold values from 0.1 to 1.9
- w_query: bfloat16 [1536, 512], replicated
- w_key: bfloat16 [1536, 128], replicated
- w_value: bfloat16 [1536, 128], replicated, may hold values from -0.15625 to 0.15625
- w_out: bfloat16 [512, 1536], replicated, may hold values from -0.25 to 0.25
Outputs:
- block_out: bfloat16 [8192, 1536], P(('dp', 'seq')), parts along dimension 0
The draws below stay inside these ranges and needn't reach their ends.
There are 4 independent parts, one for each index of `dp`. The reference program is written for one: setup_inputs(seed, part) draws one part's arguments, and reference() takes and returns one part's arrays. A program takes and returns all parts, laid end to end along the dimension named above; an argument that names none is the same for every part. Nothing has to cross between parts.
All inputs are finite; a program needn't handle non-finite values.
Results may differ from the reference program's by a relative error of at most 0.0059.
Values may be sent and summed in bfloat16 or wider, within the bound.
No kernel may reach another device: no remote copies, remote signals or barrier semaphores. Data moves between devices by JAX's collectives and lax.ppermute only.
A program may use at most 128 MiB of HBM per device.

```python
import math
import jax
import jax.numpy as jnp
from jax import lax

C = 1536
CO = 768
HEADS = 4
DH = 128
KERNEL_TAPS = 3
DILATION_STEP = 4
SEQUENCE_TOKENS = 2048


def key_matrix(key):
    draw_base = jax.random.normal(jax.random.fold_in(key, 7), (C, DH), jnp.float32)
    return jnp.clip(draw_base, -6.0, 6.0) / math.sqrt(C)


def draw_w_key(key, part):
    return key_matrix(key).astype(jnp.bfloat16)


def draw_w_query(key, part):
    draw_base = jax.random.normal(jax.random.fold_in(key, 13), (C, HEADS * DH), jnp.float32)
    draw_base = jnp.clip(draw_base, -4.0, 4.0) * (3.0 / math.sqrt(C))
    return draw_base.astype(jnp.bfloat16)


def steps_of(stream_key, shape, split, low, top_value):
    def one(axis_at, shards_of):
        heights = jax.random.uniform(jax.random.fold_in(jax.random.fold_in(stream_key, 6), axis_at), (shards_of,), jnp.float32, low / len(split), top_value / len(split))
        return jnp.repeat(jnp.exp(heights), shape[axis_at] // shards_of).reshape((-1,) + (1,) * (len(shape) - axis_at - 1))

    gain = one(*split[0])
    for cut in split[1:]:
        gain = gain * one(*cut)
    return gain


def bell_draw(key, shape, scale, most, shards=(), dtype=jnp.bfloat16):
    array = scale * jax.random.normal(key, shape, jnp.float32)
    if shards:
        array = array * steps_of(key, shape, shards, -0.22, 0.18)
    return jnp.clip(array, -most, most).astype(dtype)


def setup_inputs(seed: int = 0, part: int = 0) -> dict:
    key_of = jax.random.split(jax.random.key(seed), 10)
    own_keys = jax.random.split(jax.random.fold_in(key_of[9], part), 10)
    seq_in = bell_draw(own_keys[0], (SEQUENCE_TOKENS, C), 1.0, 6.0, ((0, 8),))
    conv_gain = jnp.clip(1.0 + 0.18 * jax.random.normal(key_of[1], (C,), jnp.float32), 0.1, 1.9)
    convolution_weight = bell_draw(key_of[2], (KERNEL_TAPS, C, CO), (KERNEL_TAPS * C) ** -0.5, 0.09375)
    conv_bias = bell_draw(key_of[3], (CO,), 0.5, 3.0, (), jnp.float32)
    attn_gain = jnp.clip(1.0 + 0.18 * jax.random.normal(key_of[4], (C,), jnp.float32), 0.1, 1.9)
    w_query = draw_w_query(jax.random.fold_in(key_of[9], 71), part)
    w_key = draw_w_key(jax.random.fold_in(key_of[9], 71), part)
    w_value = bell_draw(key_of[7], (C, DH), C ** -0.5, 0.15625)
    w_out = bell_draw(key_of[8], (HEADS * DH, C), (HEADS * DH) ** -0.5, 0.25)
    return {"seq_in": seq_in, "conv_gain": conv_gain, "convolution_weight": convolution_weight, "conv_bias": conv_bias, "attn_gain": attn_gain, "w_query": w_query, "w_key": w_key, "w_value": w_value, "w_out": w_out}


def normalize(values, gain_vec):
    wide = values.astype(jnp.float32)
    meansq = lax.optimization_barrier(jnp.mean(wide * wide, axis=-1, keepdims=True))
    return wide * lax.rsqrt(meansq + 1e-06) * gain_vec

def reference(seq_in, conv_gain, convolution_weight, conv_bias, attn_gain, w_query, w_key, w_value, w_out):
    receptive_reach = DILATION_STEP * (KERNEL_TAPS - 1) // 2
    normed = normalize(seq_in, conv_gain).astype(jnp.bfloat16)
    padded_tokens = jnp.pad(normed, ((receptive_reach, receptive_reach), (0, 0)))
    convolved_total = jnp.zeros((SEQUENCE_TOKENS, CO), jnp.float32)
    for tap_index in range(KERNEL_TAPS):
        convolved_total = convolved_total + jnp.dot(padded_tokens[tap_index * DILATION_STEP:tap_index * DILATION_STEP + SEQUENCE_TOKENS], convolution_weight[tap_index], preferred_element_type=jnp.float32)
    activated = jax.nn.gelu(convolved_total + conv_bias, approximate=True)
    wide_in = seq_in.astype(jnp.float32)
    hidden = jnp.concatenate([wide_in[:, :CO] + activated, wide_in[:, CO:]], axis=1).astype(jnp.bfloat16)
    attn_in = normalize(hidden, attn_gain).astype(jnp.bfloat16)
    queries = jnp.dot(attn_in, w_query, preferred_element_type=jnp.float32).astype(jnp.bfloat16)
    keys = jnp.dot(attn_in, w_key, preferred_element_type=jnp.float32).astype(jnp.bfloat16)
    values = jnp.dot(attn_in, w_value, preferred_element_type=jnp.float32).astype(jnp.bfloat16)
    key_wide = keys.astype(jnp.float32)
    value_wide = values.astype(jnp.float32)
    block_len = math.gcd(SEQUENCE_TOKENS, 512)
    query_blocks = queries.reshape(SEQUENCE_TOKENS // block_len, block_len, HEADS, DH)

    def attend(query_block):
        scores = jnp.einsum('thd,kd->htk', query_block.astype(jnp.float32), key_wide) * DH ** (-0.5)
        top_score = lax.optimization_barrier(jnp.max(scores, axis=-1, keepdims=True))
        expd = jnp.exp(scores - top_score)
        totals = lax.optimization_barrier(jnp.sum(expd, axis=-1))
        weights = expd.astype(jnp.bfloat16).astype(jnp.float32)
        summed = jnp.einsum('htk,kd->htd', weights, value_wide)
        result = summed / totals[..., None]
        return jnp.transpose(result, (1, 0, 2)).reshape(block_len, HEADS * DH)
    attended = lax.map(attend, query_blocks).reshape(SEQUENCE_TOKENS, HEADS * DH).astype(jnp.bfloat16)
    mixed = hidden.astype(jnp.float32) + jnp.dot(attended, w_out, preferred_element_type=jnp.float32)
    return mixed.astype(jnp.bfloat16)
```

```python
import functools

import jax
import jax.numpy as jnp
from jax import lax
from jax.experimental import pallas as pl
from jax.experimental.pallas import tpu as pltpu
from jax.sharding import PartitionSpec as P

DILATION_STEP = 4
EPS = 1e-06
LOG2E = 1.4426950408889634
F32 = jnp.float32
BF16 = jnp.bfloat16
VMEM = pl.BlockSpec(memory_space=pltpu.VMEM)
SMEM = pl.BlockSpec(memory_space=pltpu.SMEM)


def normed_rows(values, gain):
    wide = values.astype(F32)
    meansq = jnp.mean(wide * wide, axis=-1, keepdims=True)
    return wide * lax.rsqrt(meansq + EPS) * gain


def dot(a, b):
    return jnp.dot(a, b, preferred_element_type=F32)


def conv_kernel(reach, x_ref, gain_ref, w_ref, part_ref, pad_ref):
    rows, chan = x_ref.shape
    taps = w_ref.shape[0]
    pad_ref[0:8, :] = jnp.zeros((8, chan), F32)
    pad_ref[8 + rows : 16 + rows, :] = jnp.zeros((8, chan), F32)
    pad_ref[8 : 8 + rows, :] = normed_rows(x_ref[...], gain_ref[...])
    total = None
    for tap in range(taps):
        start = 8 - reach + tap * DILATION_STEP
        piece = dot(pad_ref[start : start + rows, :].astype(BF16), w_ref[tap])
        total = piece if total is None else total + piece
    part_ref[...] = total


def project_kernel(
    reach, place_ref, x_ref, part_ref, near_ref, far_ref, gain_ref, w_ref, bias_ref, again_ref, wk_ref, wv_ref,
    hidden_ref, attn_ref, kv_ref, sum_ref,
):
    rows, chan = x_ref.shape
    taps, _, out_chan = w_ref.shape
    head_dim = wk_ref.shape[1]
    index, count = place_ref[0], place_ref[1]
    even = lax.rem(index, 2) == 0
    near, far = near_ref[...].astype(F32), far_ref[...].astype(F32)
    left = jnp.where(even, far, near)
    right = jnp.where(even, near, far)
    row = lax.broadcasted_iota(jnp.int32, (2 * reach, 1), 0)
    left = jnp.where((row >= reach) & (index > 0), normed_rows(left, gain_ref[...]), 0.0)
    right = jnp.where((row < reach) & (index < count - 1), normed_rows(right, gain_ref[...]), 0.0)
    sum_ref[...] = part_ref[...]
    for tap in range(taps):
        shift = (tap - (taps - 1) // 2) * DILATION_STEP
        if shift < 0:
            window = left[2 * reach + shift : 2 * reach].astype(BF16)
            sum_ref[0:-shift, :] += dot(window, w_ref[tap])
        elif shift > 0:
            window = right[0:shift].astype(BF16)
            sum_ref[rows - shift : rows, :] += dot(window, w_ref[tap])
    activated = jax.nn.gelu(sum_ref[...] + bias_ref[...], approximate=True)
    first = (x_ref[:, :out_chan].astype(F32) + activated).astype(BF16)
    hidden_ref[:, :out_chan] = first
    hidden_ref[:, out_chan:] = x_ref[:, out_chan:]
    attn_in = normed_rows(hidden_ref[...], again_ref[...]).astype(BF16)
    attn_ref[...] = attn_in
    kv_ref[:, :head_dim] = dot(attn_in, wk_ref[...]).astype(BF16)
    kv_ref[:, head_dim:] = dot(attn_in, wv_ref[...]).astype(BF16)


def fold(q_of, heads, rows, head_dim, kv_refs, m_ref, l_ref, acc_ref, first):
    scale = LOG2E * head_dim**-0.5
    for h in range(heads):
        q = q_of(h)
        span = slice(h * rows, (h + 1) * rows)
        scores = [
            lax.dot_general(q, kv[:, :head_dim], (((1,), (1,)), ((), ())), preferred_element_type=F32) * scale
            for kv in kv_refs
        ]
        top = jnp.max(functools.reduce(jnp.maximum, scores), axis=-1, keepdims=True)
        if not first:
            old = m_ref[span, :]
            top = jnp.maximum(old, top)
        summed, total = None, None
        for s, kv in zip(scores, kv_refs):
            e = jnp.exp2(s - top)
            t = jnp.sum(e, axis=-1, keepdims=True)
            o = dot(e.astype(BF16), kv[:, head_dim:])
            summed = o if summed is None else summed + o
            total = t if total is None else total + t
        if not first:
            fade = jnp.exp2(old - top)
            summed = summed + acc_ref[span, :] * fade
            total = total + l_ref[span, :] * fade
        m_ref[span, :] = top
        l_ref[span, :] = total
        acc_ref[span, :] = summed


def query_kernel(attn_ref, wq_ref, kv_ref, q_ref, m_ref, l_ref, acc_ref):
    rows = attn_ref.shape[0]
    head_dim = kv_ref.shape[1] // 2
    heads = wq_ref.shape[1] // head_dim
    q_ref[...] = dot(attn_ref[...], wq_ref[...]).astype(BF16)
    fold(
        lambda h: q_ref[:, h * head_dim : (h + 1) * head_dim], heads, rows, head_dim,
        [kv_ref], m_ref, l_ref, acc_ref, True,
    )


def last_kernel(blocks, q_ref, hidden_ref, wo_ref, m0_ref, l0_ref, acc0_ref, *rest):
    kv_refs = rest[:blocks]
    out_ref, m_ref, l_ref, acc_ref = rest[blocks:]
    rows = q_ref.shape[0]
    head_dim = kv_refs[0].shape[1] // 2
    heads = q_ref.shape[1] // head_dim
    m_ref[...] = m0_ref[...]
    l_ref[...] = l0_ref[...]
    acc_ref[...] = acc0_ref[...]
    for kv in kv_refs:
        fold(
            lambda h: q_ref[:, h * head_dim : (h + 1) * head_dim], heads, rows, head_dim,
            [kv], m_ref, l_ref, acc_ref, False,
        )
    attended = jnp.concatenate(
        [(acc_ref[h * rows : (h + 1) * rows, :] / l_ref[h * rows : (h + 1) * rows, :]).astype(BF16) for h in range(heads)],
        axis=1,
    )
    out_ref[...] = (hidden_ref[...].astype(F32) + dot(attended, wo_ref[...])).astype(BF16)


def call(body, outs, args, specs=None, scratch=(), flops=0, moved=0, name=None):
    return pl.pallas_call(
        body,
        out_shape=outs,
        in_specs=specs or [VMEM] * len(args),
        out_specs=jax.tree.map(lambda _: VMEM, outs),
        scratch_shapes=scratch,
        compiler_params=pltpu.CompilerParams(vmem_limit_bytes=16 * 1024 * 1024),
        cost_estimate=pl.CostEstimate(flops=flops, bytes_accessed=moved, transcendentals=0),
        name=name,
    )(*args)


def shards(
    seq_in, conv_gain, convolution_weight, conv_bias, attn_gain, w_query, w_key, w_value, w_out
):
    rows, chan = seq_in.shape
    taps, _, out_chan = convolution_weight.shape
    head_dim = w_key.shape[1]
    heads = w_query.shape[1] // head_dim
    reach = DILATION_STEP * (taps - 1) // 2
    count = lax.axis_size("seq")
    index = lax.axis_index("seq")
    shape = jax.ShapeDtypeStruct

    edges = jnp.concatenate([seq_in[:reach], seq_in[rows - reach :]], axis=0)
    near = lax.ppermute(edges, "seq", [(i, i ^ 1) for i in range(count)])
    far_pairs = [(i, (i - 1 if i % 2 == 0 else i + 1) % count) for i in range(count)]
    far = lax.ppermute(edges, "seq", far_pairs)

    gain_row = conv_gain[None, :]
    part = call(
        functools.partial(conv_kernel, reach),
        shape((rows, out_chan), F32),
        (seq_in, gain_row, convolution_weight),
        scratch=[pltpu.VMEM((rows + 16, chan), F32)],
        flops=2 * rows * chan * out_chan * taps,
        moved=convolution_weight.size * 2,
        name="conv",
    )
    place = jnp.stack([index, jnp.int32(count)]).astype(jnp.int32)
    hidden, attn_in, kv = call(
        functools.partial(project_kernel, reach),
        (shape((rows, chan), BF16), shape((rows, chan), BF16), shape((rows, 2 * head_dim), BF16)),
        (place, seq_in, part, near, far, gain_row, convolution_weight, conv_bias[None, :], attn_gain[None, :], w_key, w_value),
        specs=[SMEM] + [VMEM] * 10,
        scratch=[pltpu.VMEM((rows, out_chan), F32)],
        flops=2 * rows * chan * 2 * head_dim,
        name="project",
    )
    sibling = [(i, i ^ 1) for i in range(count)]
    blocks = []
    for step in range(2, count, 2):
        blocks.append(lax.ppermute(kv, "seq", [(i, i ^ step) for i in range(count)]))
    passed = [lax.ppermute(b, "seq", sibling) for b in [kv] + blocks]
    state = (
        shape((rows * heads, 1), F32),
        shape((rows * heads, 1), F32),
        shape((rows * heads, head_dim), F32),
    )
    q, m, l, acc = call(
        query_kernel,
        (shape((rows, heads * head_dim), BF16),) + state,
        (attn_in, w_query, kv),
        flops=2 * rows * chan * heads * head_dim,
        name="query",
    )
    kvs = blocks + passed
    return call(
        functools.partial(last_kernel, len(kvs)),
        shape((rows, chan), BF16),
        (q, hidden, w_out, m, l, acc, *kvs),
        scratch=[pltpu.VMEM(s.shape, s.dtype) for s in state],
        flops=4 * rows * heads * head_dim * rows * len(kvs),
        name="attend",
    )


def solution(mesh):
    placed = (P(("dp", "seq"), None), P(), P(), P(), P(), P(), P(), P(), P())
    return jax.shard_map(
        shards, mesh=mesh, in_specs=placed, out_specs=P(("dp", "seq"), None), check_vma=False
    )
```

```python
import functools

import jax
import jax.numpy as jnp
from jax import lax
from jax.experimental import pallas as pl
from jax.experimental.pallas import tpu as pltpu
from jax.sharding import PartitionSpec as P

DILATION_STEP = 4
EPS = 1e-06
LOADF = 8_000_000_000
LOG2E = 1.4426950408889634
F32 = jnp.float32
BF16 = jnp.bfloat16
VMEM = pl.BlockSpec(memory_space=pltpu.VMEM)
SMEM = pl.BlockSpec(memory_space=pltpu.SMEM)


def normed_rows(values, gain):
    wide = values.astype(F32)
    meansq = jnp.mean(wide * wide, axis=-1, keepdims=True)
    return wide * lax.rsqrt(meansq + EPS) * gain


def dot(a, b):
    return jnp.dot(a, b, preferred_element_type=F32)


def load_kernel(reach, x_hbm, x_ref, edges_ref, sem):
    rows = x_ref.shape[0]
    copy = pltpu.make_async_copy(x_hbm, x_ref, sem)
    copy.start()
    copy.wait()
    edges_ref[0:reach, :] = x_ref[0:reach, :]
    edges_ref[reach:, :] = x_ref[rows - reach :, :]


def conv_kernel(reach, x_ref, gain_ref, w_ref, part_ref, pad_ref):
    rows, chan = x_ref.shape
    taps = w_ref.shape[0]
    pad_ref[0:8, :] = jnp.zeros((8, chan), F32)
    pad_ref[8 + rows : 16 + rows, :] = jnp.zeros((8, chan), F32)
    pad_ref[8 : 8 + rows, :] = normed_rows(x_ref[...], gain_ref[...])
    total = None
    for tap in range(taps):
        start = 8 - reach + tap * DILATION_STEP
        piece = dot(pad_ref[start : start + rows, :].astype(BF16), w_ref[tap])
        total = piece if total is None else total + piece
    part_ref[...] = total


def project_kernel(
    reach, place_ref, x_ref, part_ref, near_ref, far_ref, gain_ref, w_ref, bias_ref, again_ref, wk_ref, wv_ref,
    hidden_ref, attn_ref, kv_ref, sum_ref,
):
    rows, chan = x_ref.shape
    taps, _, out_chan = w_ref.shape
    head_dim = wk_ref.shape[1]
    index, count = place_ref[0], place_ref[1]
    even = lax.rem(index, 2) == 0
    near, far = near_ref[...].astype(F32), far_ref[...].astype(F32)
    left = jnp.where(even, far, near)
    right = jnp.where(even, near, far)
    row = lax.broadcasted_iota(jnp.int32, (2 * reach, 1), 0)
    left = jnp.where((row >= reach) & (index > 0), normed_rows(left, gain_ref[...]), 0.0)
    right = jnp.where((row < reach) & (index < count - 1), normed_rows(right, gain_ref[...]), 0.0)
    sum_ref[...] = part_ref[...]
    for tap in range(taps):
        shift = (tap - (taps - 1) // 2) * DILATION_STEP
        if shift < 0:
            window = left[2 * reach + shift : 2 * reach].astype(BF16)
            sum_ref[0:-shift, :] += dot(window, w_ref[tap])
        elif shift > 0:
            window = right[0:shift].astype(BF16)
            sum_ref[rows - shift : rows, :] += dot(window, w_ref[tap])
    activated = jax.nn.gelu(sum_ref[...] + bias_ref[...], approximate=True)
    first = (x_ref[:, :out_chan].astype(F32) + activated).astype(BF16)
    hidden_ref[:, :out_chan] = first
    hidden_ref[:, out_chan:] = x_ref[:, out_chan:]
    attn_in = normed_rows(hidden_ref[...], again_ref[...]).astype(BF16)
    attn_ref[...] = attn_in
    kv_ref[:, :head_dim] = dot(attn_in, wk_ref[...]).astype(BF16)
    kv_ref[:, head_dim:] = dot(attn_in, wv_ref[...]).astype(BF16)


def fold(q_ref, kv_refs, m_in, acc_in, m_out, acc_out):
    many, head_dim = q_ref.shape
    step = min(128, many)
    mates = [
        jnp.concatenate([kv[:, head_dim:], jnp.ones((kv.shape[0], head_dim), BF16)], axis=1) for kv in kv_refs
    ]
    for at in range(0, many, step):
        span = slice(at, at + step)
        q = q_ref[span, :]
        scores = [
            lax.dot_general(q, kv[:, :head_dim], (((1,), (1,)), ((), ())), preferred_element_type=F32)
            for kv in kv_refs
        ]
        top = jnp.max(functools.reduce(jnp.maximum, scores), axis=-1, keepdims=True)
        top = jnp.broadcast_to(top, (step, head_dim))
        if m_in is not None:
            old = m_in[span, :]
            top = jnp.maximum(old, top)
            fade = jnp.exp2(old - top)
        summed = None
        for s, mate in zip(scores, mates):
            e = jnp.exp2(s - jnp.concatenate([top] * (s.shape[1] // head_dim), axis=1))
            o = dot(e.astype(BF16), mate)
            summed = o if summed is None else summed + o
        if m_in is not None:
            summed = summed + acc_in[span, :] * jnp.concatenate([fade, fade], axis=1)
        m_out[span, :] = top
        acc_out[span, :] = summed


def query_kernel(blocks, attn_ref, wq_ref, *rest):
    kv_refs = rest[:blocks]
    q_ref, m_ref, acc_ref = rest[blocks:]
    rows = attn_ref.shape[0]
    head_dim = q_ref.shape[1]
    scale = LOG2E * head_dim**-0.5
    q = dot(attn_ref[...], wq_ref[...])
    for h in range(wq_ref.shape[1] // head_dim):
        q_ref[h * rows : (h + 1) * rows, :] = (q[:, h * head_dim : (h + 1) * head_dim] * scale).astype(BF16)
    fold(q_ref, kv_refs, None, None, m_ref, acc_ref)


def more_kernel(blocks, q_ref, m_in, acc_in, *rest):
    m_ref, acc_ref = rest[blocks:]
    fold(q_ref, rest[:blocks], m_in, acc_in, m_ref, acc_ref)


def last_kernel(blocks, q_ref, m_in, acc_in, hidden_ref, wo_ref, *rest):
    out_ref, m_ref, acc_ref = rest[blocks:]
    fold(q_ref, rest[:blocks], m_in, acc_in, m_ref, acc_ref)
    rows = hidden_ref.shape[0]
    many, head_dim = q_ref.shape
    attended = jnp.concatenate(
        [
            (acc_ref[at : at + rows, :head_dim] / acc_ref[at : at + rows, head_dim:]).astype(BF16)
            for at in range(0, many, rows)
        ],
        axis=1,
    )
    out_ref[...] = (hidden_ref[...].astype(F32) + dot(attended, wo_ref[...])).astype(BF16)


def call(body, outs, args, specs=None, scratch=(), flops=0, moved=0, name=None, alias=None):
    return pl.pallas_call(
        body,
        out_shape=outs,
        in_specs=specs or [VMEM] * len(args),
        out_specs=jax.tree.map(lambda _: VMEM, outs),
        scratch_shapes=scratch,
        input_output_aliases=alias or {},
        compiler_params=pltpu.CompilerParams(vmem_limit_bytes=16 * 1024 * 1024),
        cost_estimate=pl.CostEstimate(flops=flops, bytes_accessed=moved, transcendentals=0),
        name=name,
    )(*args)


def shards(
    seq_in, conv_gain, convolution_weight, conv_bias, attn_gain, w_query, w_key, w_value, w_out
):
    rows, chan = seq_in.shape
    taps, _, out_chan = convolution_weight.shape
    head_dim = w_key.shape[1]
    heads = w_query.shape[1] // head_dim
    reach = DILATION_STEP * (taps - 1) // 2
    count = lax.axis_size("seq")
    index = lax.axis_index("seq")
    shape = jax.ShapeDtypeStruct

    seq_in, edges = call(
        functools.partial(load_kernel, reach),
        (shape((rows, chan), BF16), shape((2 * reach, chan), BF16)),
        (seq_in,),
        specs=[pl.BlockSpec(memory_space=pltpu.HBM)],
        scratch=[pltpu.SemaphoreType.DMA],
        flops=LOADF,
        moved=rows * chan * 4,
        name="load",
    )
    near = lax.ppermute(edges, "seq", [(i, i ^ 1) for i in range(count)])
    far_pairs = [(i, (i - 1 if i % 2 == 0 else i + 1) % count) for i in range(count)]
    far = lax.ppermute(edges, "seq", far_pairs)

    gain_row = conv_gain
    part = call(
        functools.partial(conv_kernel, reach),
        shape((rows, out_chan), F32),
        (seq_in, gain_row, convolution_weight),
        scratch=[pltpu.VMEM((rows + 16, chan), F32)],
        flops=2 * rows * chan * out_chan * taps,
        moved=convolution_weight.size * 2,
        name="conv",
    )
    place = jnp.stack([index, jnp.int32(count)]).astype(jnp.int32)
    hidden, attn_in, kv = call(
        functools.partial(project_kernel, reach),
        (shape((rows, chan), BF16), shape((rows, chan), BF16), shape((rows, 2 * head_dim), BF16)),
        (place, seq_in, part, near, far, gain_row, convolution_weight, conv_bias, attn_gain, w_key, w_value),
        specs=[SMEM] + [VMEM] * 10,
        scratch=[pltpu.VMEM((rows, out_chan), F32)],
        flops=2 * rows * chan * 2 * head_dim,
        name="project",
    )
    sibling = [(i, i ^ 1) for i in range(count)]
    steps = list(range(2, count, 2))
    blocks = [lax.ppermute(kv, "seq", [(i, i ^ s) for i in range(count)]) for s in steps]
    mate = lax.ppermute(kv, "seq", sibling)
    fold_flops = 4 * rows * rows * heads * head_dim
    state = (shape((rows * heads, head_dim), F32), shape((rows * heads, 2 * head_dim), F32))
    q, m, acc = call(
        functools.partial(query_kernel, 2),
        (shape((rows * heads, head_dim), BF16),) + state,
        (attn_in, w_query, kv, mate),
        flops=2 * rows * chan * heads * head_dim + 2 * fold_flops,
        name="query",
    )
    m, acc, *near_blocks = lax.optimization_barrier((m, acc, *blocks[:-1]))
    last_block = blocks[-1]
    passed = [lax.ppermute(b, "seq", sibling) for b in near_blocks]
    m, acc = call(
        functools.partial(more_kernel, len(near_blocks)),
        state,
        (q, m, acc, *near_blocks),
        alias={1: 0, 2: 1},
        flops=len(near_blocks) * fold_flops,
        name="near",
    )
    m, acc, last_block = lax.optimization_barrier((m, acc, last_block))
    last_passed = lax.ppermute(last_block, "seq", sibling)
    middle = passed + [last_block]
    m, acc = call(
        functools.partial(more_kernel, len(middle)),
        state,
        (q, m, acc, *middle),
        alias={1: 0, 2: 1},
        flops=len(middle) * fold_flops,
        name="middle",
    )
    return call(
        functools.partial(last_kernel, 1),
        shape((rows, chan), BF16),
        (q, m, acc, hidden, w_out, last_passed),
        scratch=[pltpu.VMEM(s.shape, s.dtype) for s in state],
        flops=fold_flops + 2 * rows * chan * heads * head_dim,
        name="last",
    )


def solution(mesh):
    placed = (P(("dp", "seq"), None), P(), P(), P(), P(), P(), P(), P(), P())
    return jax.shard_map(
        shards, mesh=mesh, in_specs=placed, out_specs=P(("dp", "seq"), None), check_vma=False
    )
```

```python
import functools

import jax
import jax.numpy as jnp
from jax import lax
from jax.experimental import pallas as pl
from jax.experimental.pallas import tpu as pltpu
from jax.sharding import PartitionSpec as P

DILATION_STEP = 4
EPS = 1e-06
LOADF = 8_000_000_000
LOG2E = 1.4426950408889634
F32 = jnp.float32
BF16 = jnp.bfloat16
VMEM = pl.BlockSpec(memory_space=pltpu.VMEM)
SMEM = pl.BlockSpec(memory_space=pltpu.SMEM)


def normed_rows(values, gain):
    wide = values.astype(F32)
    meansq = jnp.mean(wide * wide, axis=-1, keepdims=True)
    return wide * lax.rsqrt(meansq + EPS) * gain


def dot(a, b):
    return jnp.dot(a, b, preferred_element_type=F32)


def edge_kernel(reach, x_hbm, edges_ref, near_ref, sems):
    rows = x_hbm.shape[0]
    tile = near_ref.shape[1]
    copies = [
        pltpu.make_async_copy(x_hbm.at[0:tile, :], near_ref.at[0], sems.at[0]),
        pltpu.make_async_copy(x_hbm.at[rows - tile : rows, :], near_ref.at[1], sems.at[1]),
    ]
    for copy in copies:
        copy.start()
    for copy in copies:
        copy.wait()
    edges_ref[0:reach, :] = near_ref[0, 0:reach, :]
    edges_ref[reach:, :] = near_ref[1, tile - reach :, :]


def center_kernel(center, x_ref, gain_ref, w_ref, normed_ref, part_ref):
    normed_ref[...] = normed_rows(x_ref[...], gain_ref[...]).astype(BF16)
    part_ref[...] = dot(normed_ref[...], w_ref[center])


def project_kernel(
    reach, x_ref, normed_ref, part_ref, near_ref, far_ref, gain_ref, w_ref, bias_ref, again_ref, wk_ref, wv_ref,
    hidden_ref, attn_ref, kv_ref, line_ref, sum_ref, *shift_refs,
):
    rows, chan = x_ref.shape
    taps, _, out_chan = w_ref.shape
    head_dim = wk_ref.shape[1]
    index, count = lax.axis_index("seq"), lax.axis_size("seq")
    even = lax.rem(index, 2) == 0
    near, far = near_ref[...].astype(F32), far_ref[...].astype(F32)
    left = jnp.where(even, far, near)
    right = jnp.where(even, near, far)
    row = lax.broadcasted_iota(jnp.int32, (2 * reach, 1), 0)
    left = jnp.where((row >= reach) & (index > 0), normed_rows(left, gain_ref[...]), 0.0)
    right = jnp.where((row < reach) & (index < count - 1), normed_rows(right, gain_ref[...]), 0.0)
    line_ref[0:rows, :] = normed_ref[...]
    line_ref[rows:, :] = jnp.concatenate([left, right], axis=0).astype(BF16)
    total = part_ref[...]
    slots = iter(shift_refs)
    for tap in range(taps):
        shift = (tap - (taps - 1) // 2) * DILATION_STEP
        if shift == 0:
            continue
        product = dot(line_ref[...], w_ref[tap])
        shift_ref = next(slots)
        if shift < 0:
            shift_ref[0 : 2 * reach, :] = product[rows : rows + 2 * reach]
            shift_ref[2 * reach :, :] = product[0:rows]
            total = total + shift_ref[2 * reach + shift : 2 * reach + shift + rows, :]
        else:
            shift_ref[0:rows, :] = product[0:rows]
            shift_ref[rows:, :] = product[rows + 2 * reach : rows + 4 * reach]
            total = total + shift_ref[shift : shift + rows, :]
    activated = jax.nn.gelu(total + bias_ref[...], approximate=True)
    hidden_ref[:, :out_chan] = (x_ref[:, :out_chan].astype(F32) + activated).astype(BF16)
    hidden_ref[:, out_chan:] = x_ref[:, out_chan:]
    attn_ref[...] = normed_rows(hidden_ref[...], again_ref[...]).astype(BF16)
    kv_ref[:, :head_dim] = dot(attn_ref[...], wk_ref[...]).astype(BF16)
    kv_ref[:, head_dim:] = dot(attn_ref[...], wv_ref[...]).astype(BF16)


def fold(q_ref, kv_refs, m_in, acc_in, m_out, acc_out):
    many, head_dim = q_ref.shape
    step = min(128, many)
    mates = [
        jnp.concatenate([kv[:, head_dim:], jnp.ones((kv.shape[0], head_dim), BF16)], axis=1) for kv in kv_refs
    ]
    for at in range(0, many, step):
        span = slice(at, at + step)
        q = q_ref[span, :]
        scores = [
            lax.dot_general(q, kv[:, :head_dim], (((1,), (1,)), ((), ())), preferred_element_type=F32)
            for kv in kv_refs
        ]
        top = jnp.max(functools.reduce(jnp.maximum, scores), axis=-1, keepdims=True)
        top = jnp.broadcast_to(top, (step, head_dim))
        if m_in is not None:
            old = m_in[span, :]
            top = jnp.maximum(old, top)
            fade = jnp.exp2(old - top)
        summed = None
        for s, mate in zip(scores, mates):
            e = jnp.exp2(s - jnp.concatenate([top] * (s.shape[1] // head_dim), axis=1))
            o = dot(e.astype(BF16), mate)
            summed = o if summed is None else summed + o
        if m_in is not None:
            summed = summed + acc_in[span, :] * jnp.concatenate([fade, fade], axis=1)
        m_out[span, :] = top
        acc_out[span, :] = summed


def query_kernel(blocks, attn_ref, wq_ref, *rest):
    kv_refs = rest[:blocks]
    q_ref, m_ref, acc_ref = rest[blocks:]
    rows = attn_ref.shape[0]
    head_dim = q_ref.shape[1]
    scale = LOG2E * head_dim**-0.5
    q = dot(attn_ref[...], wq_ref[...])
    for h in range(wq_ref.shape[1] // head_dim):
        q_ref[h * rows : (h + 1) * rows, :] = (q[:, h * head_dim : (h + 1) * head_dim] * scale).astype(BF16)
    fold(q_ref, kv_refs, None, None, m_ref, acc_ref)


def more_kernel(blocks, q_ref, m_in, acc_in, *rest):
    m_ref, acc_ref = rest[blocks:]
    fold(q_ref, rest[:blocks], m_in, acc_in, m_ref, acc_ref)


def last_kernel(blocks, q_ref, m_in, acc_in, hidden_ref, wo_ref, *rest):
    out_hbm, m_ref, acc_ref, out_ref, sems = rest[blocks:]
    fold(q_ref, rest[:blocks], m_in, acc_in, m_ref, acc_ref)
    rows = hidden_ref.shape[0]
    many, head_dim = q_ref.shape
    step = rows // sems.shape[0]
    copies = []
    for i in range(sems.shape[0]):
        span = slice(i * step, (i + 1) * step)
        attended = jnp.concatenate(
            [
                (
                    acc_ref[at + i * step : at + (i + 1) * step, :head_dim]
                    / acc_ref[at + i * step : at + (i + 1) * step, head_dim:]
                ).astype(BF16)
                for at in range(0, many, rows)
            ],
            axis=1,
        )
        out_ref[span, :] = (hidden_ref[span, :].astype(F32) + dot(attended, wo_ref[...])).astype(BF16)
        copies.append(pltpu.make_async_copy(out_ref.at[span, :], out_hbm.at[span, :], sems.at[i]))
        copies[-1].start()
    for copy in copies:
        copy.wait()


def call(body, outs, args, specs=None, scratch=(), flops=0, moved=0, name=None, alias=None, out_spec=VMEM):
    return pl.pallas_call(
        body,
        out_shape=outs,
        in_specs=specs or [VMEM] * len(args),
        out_specs=jax.tree.map(lambda _: out_spec, outs),
        scratch_shapes=scratch,
        input_output_aliases=alias or {},
        compiler_params=pltpu.CompilerParams(vmem_limit_bytes=16 * 1024 * 1024),
        cost_estimate=pl.CostEstimate(flops=flops, bytes_accessed=moved, transcendentals=0),
        name=name,
    )(*args)


def shards(
    seq_in, conv_gain, convolution_weight, conv_bias, attn_gain, w_query, w_key, w_value, w_out
):
    rows, chan = seq_in.shape
    taps, _, out_chan = convolution_weight.shape
    head_dim = w_key.shape[1]
    heads = w_query.shape[1] // head_dim
    reach = DILATION_STEP * (taps - 1) // 2
    count = lax.axis_size("seq")
    shape = jax.ShapeDtypeStruct

    edges = call(
        functools.partial(edge_kernel, reach),
        shape((2 * reach, chan), BF16),
        (pltpu.with_memory_space_constraint(seq_in, pltpu.HBM),),
        specs=[pl.BlockSpec(memory_space=pltpu.HBM)],
        scratch=[pltpu.VMEM((2, 16, chan), BF16), pltpu.SemaphoreType.DMA((2,))],
        flops=LOADF,
        moved=rows * chan * 4,
        name="edges",
    )
    near = lax.ppermute(edges, "seq", [(i, i ^ 1) for i in range(count)])
    far_pairs = [(i, (i - 1 if i % 2 == 0 else i + 1) % count) for i in range(count)]
    far = lax.ppermute(edges, "seq", far_pairs)

    normed, part = call(
        functools.partial(center_kernel, (taps - 1) // 2),
        (shape((rows, chan), BF16), shape((rows, out_chan), F32)),
        (seq_in, conv_gain, convolution_weight),
        flops=2 * rows * chan * out_chan,
        moved=rows * chan * 4 + chan * out_chan * 2,
        name="center",
    )
    hidden, attn_in, kv = call(
        functools.partial(project_kernel, reach),
        (shape((rows, chan), BF16), shape((rows, chan), BF16), shape((rows, 2 * head_dim), BF16)),
        (
            seq_in, normed, part, near, far, conv_gain, convolution_weight, conv_bias, attn_gain, w_key, w_value,
        ),
        scratch=[pltpu.VMEM((rows + 4 * reach, chan), BF16), pltpu.VMEM((rows, out_chan), F32)]
        + [pltpu.VMEM((rows + 2 * reach, out_chan), F32)] * (taps - 1),
        flops=2 * rows * chan * (2 * head_dim + (taps - 1) * out_chan),
        moved=(taps - 1) * chan * out_chan * 2,
        name="project",
    )
    sibling = [(i, i ^ 1) for i in range(count)]
    steps = list(range(2, count, 2))
    blocks = []
    for k, step in enumerate(steps):
        other = steps[k ^ 1] if (k ^ 1) < len(steps) else step
        blocks.append(lax.ppermute(kv, "seq", [(i, i ^ (step, other)[i % 2]) for i in range(count)]))
    mate = lax.ppermute(kv, "seq", sibling)
    fold_flops = 4 * rows * rows * heads * head_dim
    state = (shape((rows * heads, head_dim), F32), shape((rows * heads, 2 * head_dim), F32))
    q, m, acc = call(
        functools.partial(query_kernel, 1),
        (shape((rows * heads, head_dim), BF16),) + state,
        (attn_in, w_query, kv),
        flops=2 * rows * chan * heads * head_dim + fold_flops,
        name="query",
    )
    m, acc, *near_blocks = lax.optimization_barrier((m, acc, *blocks[:-1]))
    last_block = blocks[-1]
    passed = [lax.ppermute(b, "seq", sibling) for b in near_blocks]
    m, acc = call(
        functools.partial(more_kernel, len(near_blocks) + 1),
        state,
        (q, m, acc, mate, *near_blocks),
        alias={1: 0, 2: 1},
        flops=(len(near_blocks) + 1) * fold_flops,
        name="near",
    )
    m, acc, last_block = lax.optimization_barrier((m, acc, last_block))
    last_passed = lax.ppermute(last_block, "seq", sibling)
    middle = passed + [last_block]
    m, acc = call(
        functools.partial(more_kernel, len(middle)),
        state,
        (q, m, acc, *middle),
        alias={1: 0, 2: 1},
        flops=len(middle) * fold_flops,
        name="middle",
    )
    return call(
        functools.partial(last_kernel, 1),
        shape((rows, chan), BF16),
        (q, m, acc, hidden, w_out, last_passed),
        out_spec=pl.BlockSpec(memory_space=pltpu.HBM),
        scratch=[pltpu.VMEM(s.shape, s.dtype) for s in state]
        + [pltpu.VMEM((rows, chan), BF16), pltpu.SemaphoreType.DMA((2,))],
        flops=fold_flops + 2 * rows * chan * heads * head_dim,
        name="last",
    )


def solution(mesh):
    placed = (P(("dp", "seq"), None), P(), P(), P(), P(), P(), P(), P(), P())
    return jax.shard_map(
        shards, mesh=mesh, in_specs=placed, out_specs=P(("dp", "seq"), None), check_vma=False
    )
```

```python
import functools
import math

import jax
import jax.numpy as jnp
from jax import lax
from jax.experimental import pallas as pl
from jax.experimental.pallas import tpu as pltpu
from jax.sharding import PartitionSpec as P

DILATION_STEP = 4
EPS = 1e-06
CEILING = 100.0
LIMIT = 60
LOADF = 8_000_000_000
LOG2E = 1.4426950408889634
F32 = jnp.float32
BF16 = jnp.bfloat16
VMEM = pl.BlockSpec(memory_space=pltpu.VMEM)
SMEM = pl.BlockSpec(memory_space=pltpu.SMEM)


def normed_rows(values, gain):
    wide = values.astype(F32)
    meansq = jnp.mean(wide * wide, axis=-1, keepdims=True)
    return wide * lax.rsqrt(meansq + EPS) * gain


def dot(a, b):
    return jnp.dot(a, b, preferred_element_type=F32)


def edge_kernel(reach, x_hbm, edges_ref, near_ref, sems):
    rows = x_hbm.shape[0]
    tile = near_ref.shape[1]
    copies = [
        pltpu.make_async_copy(x_hbm.at[0:tile, :], near_ref.at[0], sems.at[0]),
        pltpu.make_async_copy(x_hbm.at[rows - tile : rows, :], near_ref.at[1], sems.at[1]),
    ]
    for copy in copies:
        copy.start()
    for copy in copies:
        copy.wait()
    edges_ref[0:reach, :] = near_ref[0, 0:reach, :]
    edges_ref[reach:, :] = near_ref[1, tile - reach :, :]


def norm_kernel(x_ref, gain_ref, normed_ref):
    normed_ref[...] = normed_rows(x_ref[...], gain_ref[...]).astype(BF16)


def center_kernel(reach, normed_ref, w_ref, part_ref, *shift_refs):
    rows = normed_ref.shape[0]
    taps, _, out_chan = w_ref.shape
    total = dot(normed_ref[...], w_ref[(taps - 1) // 2])
    slots = iter(shift_refs)
    for tap in range(taps):
        shift = (tap - (taps - 1) // 2) * DILATION_STEP
        if shift == 0:
            continue
        shift_ref = next(slots)
        edge = shift_ref.shape[0] - rows
        first = edge if shift < 0 else 0
        shift_ref[0 if shift < 0 else rows : edge if shift < 0 else rows + edge, :] = jnp.zeros((edge, out_chan), F32)
        shift_ref[first : first + rows, :] = dot(normed_ref[...], w_ref[tap])
        total = total + shift_ref[first + shift : first + shift + rows, :]
    part_ref[...] = total


def project_kernel(
    reach, x_ref, part_ref, far_ref, near_ref, gain_ref, w_ref, bias_ref, again_ref, wk_ref, wv_ref,
    hidden_ref, attn_ref, kv_ref,
):
    rows, chan = x_ref.shape
    taps, _, out_chan = w_ref.shape
    index, count = lax.axis_index("seq"), lax.axis_size("seq")
    even = lax.rem(index, 2) == 0
    near, far = near_ref[...].astype(F32), far_ref[...].astype(F32)
    left = jnp.where(even, far, near)
    right = jnp.where(even, near, far)
    row = lax.broadcasted_iota(jnp.int32, (2 * reach, 1), 0)
    left = jnp.where((row >= reach) & (index > 0), normed_rows(left, gain_ref[...]), 0.0)
    right = jnp.where((row < reach) & (index < count - 1), normed_rows(right, gain_ref[...]), 0.0)
    around = jnp.concatenate([left, right], axis=0).astype(BF16)
    edge = 16 * pl.cdiv(reach, 16)
    top, bottom = part_ref[0:edge, :], part_ref[rows - edge :, :]
    for tap in range(taps):
        shift = (tap - (taps - 1) // 2) * DILATION_STEP
        if shift == 0:
            continue
        extra = dot(around, w_ref[tap])
        blank = jnp.zeros((edge - abs(shift), out_chan), F32)
        if shift < 0:
            top = top + jnp.concatenate([extra[2 * reach + shift : 2 * reach], blank], axis=0)
        else:
            bottom = bottom + jnp.concatenate([blank, extra[2 * reach : 2 * reach + shift]], axis=0)

    def activate(span, total):
        activated = jax.nn.gelu(total + bias_ref[...], approximate=True)
        first = (x_ref[span, :out_chan].astype(F32) + activated).astype(BF16)
        hidden = jnp.concatenate([first, x_ref[span, out_chan:]], axis=1)
        hidden_ref[span, :] = hidden
        attn_ref[span, :] = normed_rows(hidden, again_ref[...]).astype(BF16)

    activate(slice(edge, rows - edge), part_ref[edge : rows - edge, :])
    activate(slice(0, edge), top)
    activate(slice(rows - edge, rows), bottom)
    kv_ref[...] = dot(attn_ref[...], jnp.concatenate([wk_ref[...], wv_ref[...]], axis=1)).astype(BF16)


def key_side(kv, head_dim):
    rows = kv.shape[0]
    ones = (lax.broadcasted_iota(jnp.int32, (head_dim, rows), 0) == 0).astype(BF16)
    return jnp.concatenate([kv[:, :head_dim].T, ones], axis=0)


def value_side(kv, head_dim):
    return jnp.concatenate([kv[:, head_dim:], jnp.ones((kv.shape[0], head_dim), BF16)], axis=1)


def fold(q_ref, kv_refs, acc_in, acc_out):
    many, head_dim = q_ref.shape[0], q_ref.shape[1] // 2
    step = math.gcd(many, 256)
    pairs = [(key_side(kv, head_dim), value_side(kv, head_dim)) for kv in kv_refs]
    for at in range(0, many, step):
        span = slice(at, at + step)
        total = acc_in[span, :]
        for keys, values in pairs:
            weights = jnp.exp2(jnp.minimum(dot(q_ref[span, :], keys), CEILING))
            total = total + dot(weights.astype(BF16), values)
        acc_out[span, :] = total


def exact(q_ref, kv_refs, acc_out):
    many, head_dim = q_ref.shape[0], q_ref.shape[1] // 2
    step = math.gcd(many, 256)
    pairs = [(kv[:, :head_dim].T, value_side(kv, head_dim)) for kv in kv_refs]
    for at in range(0, many, step):
        span = slice(at, at + step)
        scores = [dot(q_ref[span, :head_dim], keys) for keys, _ in pairs]
        top = jnp.max(functools.reduce(jnp.maximum, scores), axis=-1, keepdims=True)
        total = None
        for s, (_, values) in zip(scores, pairs):
            piece = dot(jnp.exp2(s - top).astype(BF16), values)
            total = piece if total is None else total + piece
        acc_out[span, :] = total


def query_kernel(attn_ref, wq_ref, kv_ref, q_ref, acc_ref):
    rows = attn_ref.shape[0]
    head_dim = q_ref.shape[1] // 2
    scale = LOG2E * head_dim**-0.5
    q = dot(attn_ref[...], wq_ref[...])
    keys, values = kv_ref[:, :head_dim].T, value_side(kv_ref, head_dim)
    for h in range(wq_ref.shape[1] // head_dim):
        span = slice(h * rows, (h + 1) * rows)
        q_head = (q[:, h * head_dim : (h + 1) * head_dim] * scale).astype(BF16)
        scores = dot(q_head, keys)
        top = jnp.broadcast_to(jnp.max(scores, axis=-1, keepdims=True), (rows, head_dim)).astype(BF16)
        q_ref[span, :head_dim] = q_head
        q_ref[span, head_dim:] = -top
        top = jnp.concatenate([top.astype(F32)] * (scores.shape[1] // head_dim), axis=1)
        acc_ref[span, :] = dot(jnp.exp2(scores - top).astype(BF16), values)


def more_kernel(q_ref, acc_in, *rest):
    fold(q_ref, rest[:-1], acc_in, rest[-1])


def last_kernel(blocks, q_ref, acc_in, hidden_ref, wo_ref, *rest):
    kv_refs = rest[:blocks]
    out_hbm, acc_ref, out_ref, sems = rest[-4:]
    rows, chan = hidden_ref.shape
    many, head_dim = q_ref.shape[0], q_ref.shape[1] // 2
    width = chan // sems.shape[0]

    def finish():
        attended = jnp.concatenate(
            [
                (acc_ref[at : at + rows, :head_dim] / acc_ref[at : at + rows, head_dim:]).astype(BF16)
                for at in range(0, many, rows)
            ],
            axis=1,
        )
        copies = []
        for i in range(sems.shape[0]):
            span = slice(i * width, (i + 1) * width)
            out_ref[:, span] = (hidden_ref[:, span].astype(F32) + dot(attended, wo_ref[:, span])).astype(BF16)
            copies.append(pltpu.make_async_copy(out_ref.at[:, span], out_hbm.at[:, span], sems.at[i]))
            copies[-1].start()
        return copies

    fold(q_ref, kv_refs, acc_in, acc_ref)
    copies = finish()
    sums = acc_ref[:, head_dim:]
    good = (jnp.max(sums) <= 2.0**LIMIT) & (jnp.min(sums) >= 2.0**-LIMIT)
    for copy in copies:
        copy.wait()

    @pl.when(jnp.logical_not(good))
    def _():
        exact(q_ref, rest[:-4], acc_ref)
        for copy in finish():
            copy.wait()


def call(body, outs, args, specs=None, scratch=(), flops=0, moved=0, name=None, alias=None, out_spec=VMEM):
    return pl.pallas_call(
        body,
        out_shape=outs,
        in_specs=specs or [VMEM] * len(args),
        out_specs=jax.tree.map(lambda _: out_spec, outs),
        scratch_shapes=scratch,
        input_output_aliases=alias or {},
        compiler_params=pltpu.CompilerParams(vmem_limit_bytes=16 * 1024 * 1024),
        cost_estimate=pl.CostEstimate(flops=flops, bytes_accessed=moved, transcendentals=0),
        name=name,
    )(*args)


def shards(
    seq_in, conv_gain, convolution_weight, conv_bias, attn_gain, w_query, w_key, w_value, w_out
):
    rows, chan = seq_in.shape
    taps, _, out_chan = convolution_weight.shape
    head_dim = w_key.shape[1]
    heads = w_query.shape[1] // head_dim
    reach = DILATION_STEP * (taps - 1) // 2
    count = lax.axis_size("seq")
    shape = jax.ShapeDtypeStruct

    edges = call(
        functools.partial(edge_kernel, reach),
        shape((2 * reach, chan), BF16),
        (pltpu.with_memory_space_constraint(seq_in, pltpu.HBM),),
        specs=[pl.BlockSpec(memory_space=pltpu.HBM)],
        scratch=[pltpu.VMEM((2, 16, chan), BF16), pltpu.SemaphoreType.DMA((2,))],
        flops=LOADF,
        moved=rows * chan * 4,
        name="edges",
    )
    near = lax.ppermute(edges, "seq", [(i, i ^ 1) for i in range(count)])
    far_pairs = [(i, (i - 1 if i % 2 == 0 else i + 1) % count) for i in range(count)]
    far = lax.ppermute(edges, "seq", far_pairs)

    normed = call(norm_kernel, shape((rows, chan), BF16), (seq_in, conv_gain), flops=4 * rows * chan, name="norm")
    part = call(
        functools.partial(center_kernel, reach),
        shape((rows, out_chan), F32),
        (normed, convolution_weight),
        scratch=[pltpu.VMEM((rows + 8, out_chan), F32)] * (taps - 1),
        flops=2 * rows * chan * out_chan * taps,
        moved=rows * chan * 4 + chan * out_chan * 2,
        name="center",
    )
    hidden, attn_in, kv = call(
        functools.partial(project_kernel, reach),
        (shape((rows, chan), BF16), shape((rows, chan), BF16), shape((rows, 2 * head_dim), BF16)),
        (seq_in, part, far, near, conv_gain, convolution_weight, conv_bias, attn_gain, w_key, w_value),
        flops=2 * rows * chan * 2 * head_dim,
        name="project",
    )
    sibling = [(i, i ^ 1) for i in range(count)]
    steps = list(range(2, count, 2))
    blocks = []
    for k, step in enumerate(steps):
        other = steps[k ^ 1] if (k ^ 1) < len(steps) else step
        blocks.append(lax.ppermute(kv, "seq", [(i, i ^ (step, other)[i % 2]) for i in range(count)]))
    mate = lax.ppermute(kv, "seq", sibling)
    fold_flops = 4 * rows * rows * heads * head_dim
    q_shape, acc_shape = shape((rows * heads, 2 * head_dim), BF16), shape((rows * heads, 2 * head_dim), F32)
    q, acc = call(
        query_kernel,
        (q_shape, acc_shape),
        (attn_in, w_query, kv),
        flops=2 * rows * chan * heads * head_dim + fold_flops,
        name="query",
    )
    passed = []
    for k, block in enumerate(blocks):
        acc, block = lax.optimization_barrier((acc, block))
        blocks[k] = block
        passed.append(lax.ppermute(block, "seq", sibling))
        group = [block]
        if k == len(blocks) - 1:
            group = [mate, block, *passed[:-1]]
        acc = call(
            more_kernel,
            acc_shape,
            (q, acc, *group),
            alias={1: 0},
            flops=len(group) * fold_flops,
            name=f"fold{k}",
        )
    return call(
        functools.partial(last_kernel, 1),
        shape((rows, chan), BF16),
        (q, acc, hidden, w_out, passed[-1], *passed[:-1], kv, mate, *blocks),
        out_spec=pl.BlockSpec(memory_space=pltpu.HBM),
        scratch=[
            pltpu.VMEM(acc_shape.shape, F32),
            pltpu.VMEM((rows, chan), BF16),
            pltpu.SemaphoreType.DMA((3,)),
        ],
        flops=fold_flops + 2 * rows * chan * heads * head_dim,
        name="last",
    )


def solution(mesh):
    placed = (P(("dp", "seq"), None), P(), P(), P(), P(), P(), P(), P(), P())
    return jax.shard_map(
        shards, mesh=mesh, in_specs=placed, out_specs=P(("dp", "seq"), None), check_vma=False
    )
```

```python
import functools
import math

import jax
import jax.numpy as jnp
from jax import lax
from jax.experimental import pallas as pl
from jax.experimental.pallas import tpu as pltpu
from jax.sharding import PartitionSpec as P

DILATION_STEP = 4
EPS = 1e-06
CEILING = 100.0
LIMIT = 60
LOADF = 8_000_000_000
LOG2E = 1.4426950408889634
F32 = jnp.float32
BF16 = jnp.bfloat16
VMEM = pl.BlockSpec(memory_space=pltpu.VMEM)
SMEM = pl.BlockSpec(memory_space=pltpu.SMEM)


def normed_rows(values, gain):
    wide = values.astype(F32)
    meansq = jnp.mean(wide * wide, axis=-1, keepdims=True)
    return wide * lax.rsqrt(meansq + EPS) * gain


def dot(a, b):
    return jnp.dot(a, b, preferred_element_type=F32)


def edge_kernel(reach, x_hbm, edges_ref, near_ref, sems):
    rows = x_hbm.shape[0]
    tile = near_ref.shape[1]
    copies = [
        pltpu.make_async_copy(x_hbm.at[0:tile, :], near_ref.at[0], sems.at[0]),
        pltpu.make_async_copy(x_hbm.at[rows - tile : rows, :], near_ref.at[1], sems.at[1]),
    ]
    for copy in copies:
        copy.start()
    for copy in copies:
        copy.wait()
    edges_ref[0:reach, :] = near_ref[0, 0:reach, :]
    edges_ref[reach:, :] = near_ref[1, tile - reach :, :]


def norm_kernel(x_ref, gain_ref, normed_ref):
    normed_ref[...] = normed_rows(x_ref[...], gain_ref[...]).astype(BF16)


def center_kernel(reach, normed_ref, near_ref, gain_ref, w_ref, part_ref, *shift_refs):
    rows, chan = normed_ref.shape
    taps, _, out_chan = w_ref.shape
    total = dot(normed_ref[...], w_ref[(taps - 1) // 2])
    even = lax.rem(lax.axis_index("seq"), 2) == 0
    near = normed_rows(near_ref[...], gain_ref[...])
    row = lax.broadcasted_iota(jnp.int32, (2 * reach, 1), 0)
    left = jnp.where((row >= reach) & jnp.logical_not(even), near, 0.0)
    right = jnp.where((row < reach) & even, near, 0.0)
    line = jnp.concatenate([normed_ref[...], jnp.concatenate([left, right], axis=0).astype(BF16)], axis=0)
    slots = iter(shift_refs)
    for tap in range(taps):
        shift = (tap - (taps - 1) // 2) * DILATION_STEP
        if shift == 0:
            continue
        shift_ref = next(slots)
        product = dot(line, w_ref[tap])
        if shift < 0:
            shift_ref[0 : 2 * reach, :] = product[rows : rows + 2 * reach]
            shift_ref[2 * reach :, :] = product[0:rows]
            total = total + shift_ref[2 * reach + shift : 2 * reach + shift + rows, :]
        else:
            shift_ref[0:rows, :] = product[0:rows]
            shift_ref[rows:, :] = product[rows + 2 * reach : rows + 4 * reach]
            total = total + shift_ref[shift : shift + rows, :]
    part_ref[...] = total


def project_kernel(
    reach, x_ref, part_ref, far_ref, gain_ref, w_ref, bias_ref, again_ref, wk_ref, wv_ref,
    hidden_ref, attn_ref, kv_ref,
):
    rows, chan = x_ref.shape
    taps, _, out_chan = w_ref.shape
    index, count = lax.axis_index("seq"), lax.axis_size("seq")
    even = lax.rem(index, 2) == 0
    outside = (index == 0) | (index == count - 1)
    far = jnp.where(outside, 0.0, normed_rows(far_ref[...], gain_ref[...]))
    far = jnp.concatenate([far, jnp.zeros_like(far)], axis=0).astype(BF16)
    edge = 16 * pl.cdiv(reach, 16)
    top, bottom = part_ref[0:edge, :], part_ref[rows - edge :, :]
    middle = (taps - 1) // 2
    for away in range(1, middle + 1):
        shift = away * DILATION_STEP
        extra = dot(far, w_ref[jnp.where(even, middle - away, middle + away)])
        blank = jnp.zeros((edge - shift, out_chan), F32)
        top = top + jnp.where(even, jnp.concatenate([extra[2 * reach - shift : 2 * reach], blank], axis=0), 0.0)
        bottom = bottom + jnp.where(even, 0.0, jnp.concatenate([blank, extra[0:shift]], axis=0))

    def activate(span, total):
        activated = jax.nn.gelu(total + bias_ref[...], approximate=True)
        first = (x_ref[span, :out_chan].astype(F32) + activated).astype(BF16)
        hidden = jnp.concatenate([first, x_ref[span, out_chan:]], axis=1)
        hidden_ref[span, :] = hidden
        attn_ref[span, :] = normed_rows(hidden, again_ref[...]).astype(BF16)

    both = jnp.concatenate([wk_ref[...], wv_ref[...]], axis=1)
    for span in (slice(edge, rows // 2), slice(rows // 2, rows - edge)):
        activate(span, part_ref[span, :])
        kv_ref[span, :] = dot(attn_ref[span, :], both).astype(BF16)
    activate(slice(0, edge), top)
    activate(slice(rows - edge, rows), bottom)
    ends = jnp.concatenate([attn_ref[0:edge, :], attn_ref[rows - edge :, :]], axis=0)
    ends = dot(ends, both).astype(BF16)
    kv_ref[0:edge, :] = ends[:edge]
    kv_ref[rows - edge :, :] = ends[edge:]


def key_side(kv, head_dim):
    rows = kv.shape[0]
    ones = (lax.broadcasted_iota(jnp.int32, (head_dim, rows), 0) == 0).astype(BF16)
    return jnp.concatenate([kv[:, :head_dim].T, ones], axis=0)


def value_side(kv, head_dim):
    return jnp.concatenate([kv[:, head_dim:], jnp.ones((kv.shape[0], head_dim), BF16)], axis=1)


def fold(q_ref, kv_refs, acc_in, acc_out):
    many, head_dim = q_ref.shape[0], q_ref.shape[1] // 2
    scale = LOG2E * head_dim**-0.5
    step = math.gcd(many, 256)
    pairs = [(key_side(kv, head_dim), value_side(kv, head_dim)) for kv in kv_refs]
    for at in range(0, many, step):
        span = slice(at, at + step)
        total = acc_in[span, :]
        for keys, values in pairs:
            scores = dot(q_ref[span, :], keys) * scale
            weights = jnp.exp2(jnp.minimum(scores, CEILING))
            total = total + dot(weights.astype(BF16), values)
        acc_out[span, :] = total


def exact(q_ref, kv_refs, acc_out):
    many, head_dim = q_ref.shape[0], q_ref.shape[1] // 2
    scale = LOG2E * head_dim**-0.5
    step = math.gcd(many, 256)
    pairs = [(kv[:, :head_dim].T, value_side(kv, head_dim)) for kv in kv_refs]
    for at in range(0, many, step):
        span = slice(at, at + step)
        scores = [dot(q_ref[span, :head_dim], keys) * scale for keys, _ in pairs]
        top = jnp.max(functools.reduce(jnp.maximum, scores), axis=-1, keepdims=True)
        total = None
        for s, (_, values) in zip(scores, pairs):
            piece = dot(jnp.exp2(s - top).astype(BF16), values)
            total = piece if total is None else total + piece
        acc_out[span, :] = total


def query_kernel(attn_ref, wq_ref, kv_ref, q_ref, acc_ref):
    rows = attn_ref.shape[0]
    head_dim = q_ref.shape[1] // 2
    scale = LOG2E * head_dim**-0.5
    q = dot(attn_ref[...], wq_ref[...])
    keys, values = kv_ref[:, :head_dim].T, value_side(kv_ref, head_dim)
    for h in range(wq_ref.shape[1] // head_dim):
        span = slice(h * rows, (h + 1) * rows)
        q_head = q[:, h * head_dim : (h + 1) * head_dim].astype(BF16)
        scores = dot(q_head, keys)
        top = jnp.broadcast_to(jnp.max(scores, axis=-1, keepdims=True), (rows, head_dim)).astype(BF16)
        q_ref[span, :head_dim] = q_head
        q_ref[span, head_dim:] = -top
        top = jnp.concatenate([top.astype(F32)] * (scores.shape[1] // head_dim), axis=1)
        acc_ref[span, :] = dot(jnp.exp2((scores - top) * scale).astype(BF16), values)


def more_kernel(q_ref, acc_in, *rest):
    fold(q_ref, rest[:-1], acc_in, rest[-1])


def last_kernel(blocks, q_ref, acc_in, hidden_ref, wo_ref, *rest):
    kv_refs = rest[:blocks]
    out_hbm, acc_ref, out_ref, sems = rest[-4:]
    rows, chan = hidden_ref.shape
    many, head_dim = q_ref.shape[0], q_ref.shape[1] // 2
    width = chan // sems.shape[0]

    def finish():
        attended = jnp.concatenate(
            [
                (acc_ref[at : at + rows, :head_dim] / acc_ref[at : at + rows, head_dim:]).astype(BF16)
                for at in range(0, many, rows)
            ],
            axis=1,
        )
        copies = []
        for i in range(sems.shape[0]):
            span = slice(i * width, (i + 1) * width)
            out_ref[:, span] = (hidden_ref[:, span].astype(F32) + dot(attended, wo_ref[:, span])).astype(BF16)
            copies.append(pltpu.make_async_copy(out_ref.at[:, span], out_hbm.at[:, span], sems.at[i]))
            copies[-1].start()
        return copies

    fold(q_ref, kv_refs, acc_in, acc_ref)
    copies = finish()
    sums = acc_ref[:, head_dim:]
    good = (jnp.max(sums) <= 2.0**LIMIT) & (jnp.min(sums) >= 2.0**-LIMIT)
    for copy in copies:
        copy.wait()

    @pl.when(jnp.logical_not(good))
    def _():
        exact(q_ref, rest[:-4], acc_ref)
        for copy in finish():
            copy.wait()


def call(body, outs, args, specs=None, scratch=(), flops=0, moved=0, name=None, alias=None, out_spec=VMEM):
    return pl.pallas_call(
        body,
        out_shape=outs,
        in_specs=specs or [VMEM] * len(args),
        out_specs=jax.tree.map(lambda _: out_spec, outs),
        scratch_shapes=scratch,
        input_output_aliases=alias or {},
        compiler_params=pltpu.CompilerParams(vmem_limit_bytes=16 * 1024 * 1024),
        cost_estimate=pl.CostEstimate(flops=flops, bytes_accessed=moved, transcendentals=0),
        name=name,
    )(*args)


def shards(
    seq_in, conv_gain, convolution_weight, conv_bias, attn_gain, w_query, w_key, w_value, w_out
):
    rows, chan = seq_in.shape
    taps, _, out_chan = convolution_weight.shape
    head_dim = w_key.shape[1]
    heads = w_query.shape[1] // head_dim
    reach = DILATION_STEP * (taps - 1) // 2
    count = lax.axis_size("seq")
    shape = jax.ShapeDtypeStruct

    edges = call(
        functools.partial(edge_kernel, reach),
        shape((2 * reach, chan), BF16),
        (pltpu.with_memory_space_constraint(seq_in, pltpu.HBM),),
        specs=[pl.BlockSpec(memory_space=pltpu.HBM)],
        scratch=[pltpu.VMEM((2, 16, chan), BF16), pltpu.SemaphoreType.DMA((2,))],
        flops=LOADF,
        moved=rows * chan * 4,
        name="edges",
    )
    near = lax.ppermute(edges, "seq", [(i, i ^ 1) for i in range(count)])
    far_pairs = [(i, (i - 1 if i % 2 == 0 else i + 1) % count) for i in range(count)]
    far = lax.ppermute(edges, "seq", far_pairs)

    normed = call(norm_kernel, shape((rows, chan), BF16), (seq_in, conv_gain), flops=4 * rows * chan, name="norm")
    part = call(
        functools.partial(center_kernel, reach),
        shape((rows, out_chan), F32),
        (normed, near, conv_gain, convolution_weight),
        scratch=[pltpu.VMEM((rows + 2 * reach, out_chan), F32)] * (taps - 1),
        flops=2 * rows * chan * out_chan * taps,
        moved=rows * chan * 4 + chan * out_chan * 2,
        name="center",
    )
    hidden, attn_in, kv = call(
        functools.partial(project_kernel, reach),
        (shape((rows, chan), BF16), shape((rows, chan), BF16), shape((rows, 2 * head_dim), BF16)),
        (seq_in, part, far, conv_gain, convolution_weight, conv_bias, attn_gain, w_key, w_value),
        flops=2 * rows * chan * 2 * head_dim,
        name="project",
    )
    steps = list(range(2, count, 2))
    blocks = []
    for k, step in enumerate(steps):
        other = steps[k ^ 1] if (k ^ 1) < len(steps) else step
        blocks.append(lax.ppermute(kv, "seq", [(i, i ^ (step, other)[i % 2]) for i in range(count)]))
    sibling = [(i, i ^ 1) for i in range(count)]
    mate = lax.ppermute(kv, "seq", sibling)
    fold_flops = 4 * rows * rows * heads * head_dim
    q_shape, acc_shape = shape((rows * heads, 2 * head_dim), BF16), shape((rows * heads, 2 * head_dim), F32)
    q, acc = call(
        query_kernel,
        (q_shape, acc_shape),
        (attn_in, w_query, kv),
        flops=2 * rows * chan * heads * head_dim + fold_flops,
        name="query",
    )
    passed = []
    for k, block in enumerate(blocks):
        acc, block = lax.optimization_barrier((acc, block))
        blocks[k] = block
        passed.append(lax.ppermute(block, "seq", sibling))
        group = [block]
        if k == len(blocks) - 1:
            group = [mate, block, *passed[:-1]]
        acc = call(
            more_kernel,
            acc_shape,
            (q, acc, *group),
            alias={1: 0},
            flops=len(group) * fold_flops,
            name=f"fold{k}",
        )
    return call(
        functools.partial(last_kernel, 1),
        shape((rows, chan), BF16),
        (q, acc, hidden, w_out, passed[-1], *passed[:-1], kv, mate, *blocks),
        out_spec=pl.BlockSpec(memory_space=pltpu.HBM),
        scratch=[
            pltpu.VMEM(acc_shape.shape, F32),
            pltpu.VMEM((rows, chan), BF16),
            pltpu.SemaphoreType.DMA((3,)),
        ],
        flops=fold_flops + 2 * rows * chan * heads * head_dim,
        name="last",
    )


def solution(mesh):
    placed = (P(("dp", "seq"), None), P(), P(), P(), P(), P(), P(), P(), P())
    return jax.shard_map(
        shards, mesh=mesh, in_specs=placed, out_specs=P(("dp", "seq"), None), check_vma=False
    )
```

```python
import functools
import math

import jax
import jax.numpy as jnp
from jax import lax
from jax.experimental import pallas as pl
from jax.experimental.pallas import tpu as pltpu
from jax.sharding import PartitionSpec as P

DILATION_STEP = 4
EPS = 1e-06
CEILING = 100.0
LIMIT = 60
LOADF = 8_000_000_000
LOG2E = 1.4426950408889634
F32 = jnp.float32
BF16 = jnp.bfloat16
VMEM = pl.BlockSpec(memory_space=pltpu.VMEM)
SMEM = pl.BlockSpec(memory_space=pltpu.SMEM)


def normed_rows(values, gain):
    wide = values.astype(F32)
    meansq = jnp.mean(wide * wide, axis=-1, keepdims=True)
    return wide * lax.rsqrt(meansq + EPS) * gain


def dot(a, b):
    return jnp.dot(a, b, preferred_element_type=F32)


def edge_kernel(reach, x_hbm, near_ref, far_ref, ends_ref, sems):
    rows = x_hbm.shape[0]
    tile = ends_ref.shape[1]
    copies = [
        pltpu.make_async_copy(x_hbm.at[0:tile, :], ends_ref.at[0], sems.at[0]),
        pltpu.make_async_copy(x_hbm.at[rows - tile : rows, :], ends_ref.at[1], sems.at[1]),
    ]
    for copy in copies:
        copy.start()
    for copy in copies:
        copy.wait()
    first, last = ends_ref[0, 0:reach, :], ends_ref[1, tile - reach :, :]
    even = lax.rem(lax.axis_index("seq"), 2) == 0
    near_ref[...] = jnp.where(even, last, first)
    far_ref[...] = jnp.where(even, first, last)


def norm_kernel(x_ref, gain_ref, normed_ref):
    normed_ref[...] = normed_rows(x_ref[...], gain_ref[...]).astype(BF16)


def center_kernel(reach, normed_ref, near_ref, gain_ref, w_ref, part_ref, *shift_refs):
    rows, chan = normed_ref.shape
    taps, _, out_chan = w_ref.shape
    total = dot(normed_ref[...], w_ref[(taps - 1) // 2])
    even = lax.rem(lax.axis_index("seq"), 2) == 0
    near = normed_rows(near_ref[...], gain_ref[...])
    spare = jnp.zeros((16 * pl.cdiv(reach, 16) - reach, chan), F32)
    line = jnp.concatenate([normed_ref[...], jnp.concatenate([near, spare], axis=0).astype(BF16)], axis=0)
    blank = jnp.zeros((reach, out_chan), F32)
    slots = iter(shift_refs)
    for tap in range(taps):
        shift = (tap - (taps - 1) // 2) * DILATION_STEP
        if shift == 0:
            continue
        shift_ref = next(slots)
        product = dot(line, w_ref[tap])
        beside = product[rows : rows + reach]
        if shift < 0:
            shift_ref[0 : 2 * reach, :] = jnp.concatenate([blank, jnp.where(even, 0.0, beside)], axis=0)
            shift_ref[2 * reach :, :] = product[0:rows]
            total = total + shift_ref[2 * reach + shift : 2 * reach + shift + rows, :]
        else:
            shift_ref[0:rows, :] = product[0:rows]
            shift_ref[rows:, :] = jnp.concatenate([jnp.where(even, beside, 0.0), blank], axis=0)
            total = total + shift_ref[shift : shift + rows, :]
    part_ref[...] = total


def project_kernel(
    reach, x_ref, part_ref, far_ref, gain_ref, w_ref, bias_ref, again_ref, wk_ref, wv_ref,
    hidden_ref, attn_ref, kv_ref,
):
    rows, chan = x_ref.shape
    taps, _, out_chan = w_ref.shape
    index, count = lax.axis_index("seq"), lax.axis_size("seq")
    even = lax.rem(index, 2) == 0
    outside = (index == 0) | (index == count - 1)
    far = jnp.where(outside, 0.0, normed_rows(far_ref[...], gain_ref[...]))
    edge = 16 * pl.cdiv(reach, 16)
    far = jnp.concatenate([far, jnp.zeros((edge - reach, chan), F32)], axis=0).astype(BF16)
    top, bottom = part_ref[0:edge, :], part_ref[rows - edge :, :]
    middle = (taps - 1) // 2
    for away in range(1, middle + 1):
        shift = away * DILATION_STEP
        extra = dot(far, w_ref[jnp.where(even, middle - away, middle + away)])
        blank = jnp.zeros((edge - shift, out_chan), F32)
        top = top + jnp.where(even, jnp.concatenate([extra[reach - shift : reach], blank], axis=0), 0.0)
        bottom = bottom + jnp.where(even, 0.0, jnp.concatenate([blank, extra[0:shift]], axis=0))

    def activate(span, total):
        activated = jax.nn.gelu(total + bias_ref[...], approximate=True)
        first = (x_ref[span, :out_chan].astype(F32) + activated).astype(BF16)
        hidden = jnp.concatenate([first, x_ref[span, out_chan:]], axis=1)
        hidden_ref[span, :] = hidden
        attn_ref[span, :] = normed_rows(hidden, again_ref[...]).astype(BF16)

    both = jnp.concatenate([wk_ref[...], wv_ref[...]], axis=1)
    for span in (slice(edge, rows // 2), slice(rows // 2, rows - edge)):
        activate(span, part_ref[span, :])
        kv_ref[span, :] = dot(attn_ref[span, :], both).astype(BF16)
    activate(slice(0, edge), top)
    activate(slice(rows - edge, rows), bottom)
    ends = jnp.concatenate([attn_ref[0:edge, :], attn_ref[rows - edge :, :]], axis=0)
    ends = dot(ends, both).astype(BF16)
    kv_ref[0:edge, :] = ends[:edge]
    kv_ref[rows - edge :, :] = ends[edge:]


def key_side(kv, head_dim):
    rows = kv.shape[0]
    ones = (lax.broadcasted_iota(jnp.int32, (head_dim, rows), 0) == 0).astype(BF16)
    return jnp.concatenate([kv[:, :head_dim].T, ones], axis=0)


def value_side(kv, head_dim):
    return jnp.concatenate([kv[:, head_dim:], jnp.ones((kv.shape[0], head_dim), BF16)], axis=1)


def fold(q_ref, kv_refs, acc_in, acc_out):
    many, head_dim = q_ref.shape[0], q_ref.shape[1] // 2
    scale = LOG2E * head_dim**-0.5
    step = math.gcd(many, 256)
    pairs = [(key_side(kv, head_dim), value_side(kv, head_dim)) for kv in kv_refs]
    for at in range(0, many, step):
        span = slice(at, at + step)
        total = acc_in[span, :]
        for keys, values in pairs:
            scores = dot(q_ref[span, :], keys) * scale
            weights = jnp.exp2(jnp.minimum(scores, CEILING))
            total = total + dot(weights.astype(BF16), values)
        acc_out[span, :] = total


def exact(q_ref, kv_refs, acc_out):
    many, head_dim = q_ref.shape[0], q_ref.shape[1] // 2
    scale = LOG2E * head_dim**-0.5
    step = math.gcd(many, 256)
    pairs = [(kv[:, :head_dim].T, value_side(kv, head_dim)) for kv in kv_refs]
    for at in range(0, many, step):
        span = slice(at, at + step)
        scores = [dot(q_ref[span, :head_dim], keys) * scale for keys, _ in pairs]
        top = jnp.max(functools.reduce(jnp.maximum, scores), axis=-1, keepdims=True)
        total = None
        for s, (_, values) in zip(scores, pairs):
            piece = dot(jnp.exp2(s - top).astype(BF16), values)
            total = piece if total is None else total + piece
        acc_out[span, :] = total


def query_kernel(attn_ref, wq_ref, kv_ref, q_ref, acc_ref):
    rows = attn_ref.shape[0]
    head_dim = q_ref.shape[1] // 2
    scale = LOG2E * head_dim**-0.5
    q = dot(attn_ref[...], wq_ref[...])
    keys, values = kv_ref[:, :head_dim].T, value_side(kv_ref, head_dim)
    for h in range(wq_ref.shape[1] // head_dim):
        span = slice(h * rows, (h + 1) * rows)
        q_head = q[:, h * head_dim : (h + 1) * head_dim].astype(BF16)
        scores = dot(q_head, keys)
        top = jnp.broadcast_to(jnp.max(scores, axis=-1, keepdims=True), (rows, head_dim)).astype(BF16)
        q_ref[span, :head_dim] = q_head
        q_ref[span, head_dim:] = -top
        top = jnp.concatenate([top.astype(F32)] * (scores.shape[1] // head_dim), axis=1)
        acc_ref[span, :] = dot(jnp.exp2((scores - top) * scale).astype(BF16), values)


def more_kernel(q_ref, acc_in, *rest):
    fold(q_ref, rest[:-1], acc_in, rest[-1])


def last_kernel(blocks, q_ref, acc_in, hidden_ref, wo_ref, *rest):
    kv_refs = rest[:blocks]
    out_hbm, acc_ref, out_ref, sems = rest[-4:]
    rows, chan = hidden_ref.shape
    many, head_dim = q_ref.shape[0], q_ref.shape[1] // 2
    width = chan // sems.shape[0]

    def finish():
        attended = jnp.concatenate(
            [
                (acc_ref[at : at + rows, :head_dim] / acc_ref[at : at + rows, head_dim:]).astype(BF16)
                for at in range(0, many, rows)
            ],
            axis=1,
        )
        copies = []
        for i in range(sems.shape[0]):
            span = slice(i * width, (i + 1) * width)
            out_ref[:, span] = (hidden_ref[:, span].astype(F32) + dot(attended, wo_ref[:, span])).astype(BF16)
            copies.append(pltpu.make_async_copy(out_ref.at[:, span], out_hbm.at[:, span], sems.at[i]))
            copies[-1].start()
        return copies

    fold(q_ref, kv_refs, acc_in, acc_ref)
    copies = finish()
    sums = acc_ref[:, head_dim:]
    good = (jnp.max(sums) <= 2.0**LIMIT) & (jnp.min(sums) >= 2.0**-LIMIT)
    for copy in copies:
        copy.wait()

    @pl.when(jnp.logical_not(good))
    def _():
        exact(q_ref, rest[:-4], acc_ref)
        for copy in finish():
            copy.wait()


def call(body, outs, args, specs=None, scratch=(), flops=0, moved=0, name=None, alias=None, out_spec=VMEM):
    return pl.pallas_call(
        body,
        out_shape=outs,
        in_specs=specs or [VMEM] * len(args),
        out_specs=jax.tree.map(lambda _: out_spec, outs),
        scratch_shapes=scratch,
        input_output_aliases=alias or {},
        compiler_params=pltpu.CompilerParams(vmem_limit_bytes=16 * 1024 * 1024),
        cost_estimate=pl.CostEstimate(flops=flops, bytes_accessed=moved, transcendentals=0),
        name=name,
    )(*args)


def shards(
    seq_in, conv_gain, convolution_weight, conv_bias, attn_gain, w_query, w_key, w_value, w_out
):
    rows, chan = seq_in.shape
    taps, _, out_chan = convolution_weight.shape
    head_dim = w_key.shape[1]
    heads = w_query.shape[1] // head_dim
    reach = DILATION_STEP * (taps - 1) // 2
    count = lax.axis_size("seq")
    shape = jax.ShapeDtypeStruct

    near, far = call(
        functools.partial(edge_kernel, reach),
        (shape((reach, chan), BF16),) * 2,
        (pltpu.with_memory_space_constraint(seq_in, pltpu.HBM),),
        specs=[pl.BlockSpec(memory_space=pltpu.HBM)],
        scratch=[pltpu.VMEM((2, 16 * pl.cdiv(reach, 16), chan), BF16), pltpu.SemaphoreType.DMA((2,))],
        flops=LOADF,
        moved=rows * chan * 4,
        name="edges",
    )
    far_pairs = [(i, (i - 1 if i % 2 == 0 else i + 1) % count) for i in range(count)]
    far = lax.ppermute(far, "seq", far_pairs)
    near = lax.ppermute(near, "seq", [(i, i ^ 1) for i in range(count)])
    normed = call(norm_kernel, shape((rows, chan), BF16), (seq_in, conv_gain), flops=4 * rows * chan, name="norm")
    part = call(
        functools.partial(center_kernel, reach),
        shape((rows, out_chan), F32),
        (normed, near, conv_gain, convolution_weight),
        scratch=[pltpu.VMEM((rows + 2 * reach, out_chan), F32)] * (taps - 1),
        flops=2 * rows * chan * out_chan * taps,
        moved=rows * chan * 4 + chan * out_chan * 2,
        name="center",
    )
    hidden, attn_in, kv = call(
        functools.partial(project_kernel, reach),
        (shape((rows, chan), BF16), shape((rows, chan), BF16), shape((rows, 2 * head_dim), BF16)),
        (seq_in, part, far, conv_gain, convolution_weight, conv_bias, attn_gain, w_key, w_value),
        flops=2 * rows * chan * 2 * head_dim,
        name="project",
    )
    steps = list(range(2, count, 2))
    blocks = []
    for k, step in enumerate(steps):
        other = steps[k ^ 1] if (k ^ 1) < len(steps) else step
        blocks.append(lax.ppermute(kv, "seq", [(i, i ^ (step, other)[i % 2]) for i in range(count)]))
    sibling = [(i, i ^ 1) for i in range(count)]
    mate = lax.ppermute(kv, "seq", sibling)
    fold_flops = 4 * rows * rows * heads * head_dim
    q_shape, acc_shape = shape((rows * heads, 2 * head_dim), BF16), shape((rows * heads, 2 * head_dim), F32)
    q, acc = call(
        query_kernel,
        (q_shape, acc_shape),
        (attn_in, w_query, kv),
        flops=2 * rows * chan * heads * head_dim + fold_flops,
        name="query",
    )
    passed = []
    for k, block in enumerate(blocks):
        acc, block = lax.optimization_barrier((acc, block))
        blocks[k] = block
        passed.append(lax.ppermute(block, "seq", sibling))
        group = [block]
        if k == len(blocks) - 1:
            group = [mate, block, *passed[:-1]]
        acc = call(
            more_kernel,
            acc_shape,
            (q, acc, *group),
            alias={1: 0},
            flops=len(group) * fold_flops,
            name=f"fold{k}",
        )
    return call(
        functools.partial(last_kernel, 1),
        shape((rows, chan), BF16),
        (q, acc, hidden, w_out, passed[-1], *passed[:-1], kv, mate, *blocks),
        out_spec=pl.BlockSpec(memory_space=pltpu.HBM),
        scratch=[
            pltpu.VMEM(acc_shape.shape, F32),
            pltpu.VMEM((rows, chan), BF16),
            pltpu.SemaphoreType.DMA((3,)),
        ],
        flops=fold_flops + 2 * rows * chan * heads * head_dim,
        name="last",
    )


def solution(mesh):
    placed = (P(("dp", "seq"), None), P(), P(), P(), P(), P(), P(), P(), P())
    return jax.shard_map(
        shards, mesh=mesh, in_specs=placed, out_specs=P(("dp", "seq"), None), check_vma=False
    )
```

```python
import functools
import math

import jax
import jax.numpy as jnp
from jax import lax
from jax.experimental import pallas as pl
from jax.experimental.pallas import tpu as pltpu
from jax.sharding import PartitionSpec as P

DILATION_STEP = 4
EPS = 1e-06
CEILING = 100.0
LIMIT = 60
LOADF = 8_000_000_000
LOG2E = 1.4426950408889634
F32 = jnp.float32
BF16 = jnp.bfloat16
VMEM = pl.BlockSpec(memory_space=pltpu.VMEM)
SMEM = pl.BlockSpec(memory_space=pltpu.SMEM)


def normed_rows(values, gain):
    wide = values.astype(F32)
    meansq = jnp.mean(wide * wide, axis=-1, keepdims=True)
    return wide * lax.rsqrt(meansq + EPS) * gain


def dot(a, b):
    return jnp.dot(a, b, preferred_element_type=F32)


def edge_kernel(reach, x_hbm, near_ref, far_ref, ends_ref, sems):
    rows = x_hbm.shape[0]
    tile = ends_ref.shape[1]
    copies = [
        pltpu.make_async_copy(x_hbm.at[0:tile, :], ends_ref.at[0], sems.at[0]),
        pltpu.make_async_copy(x_hbm.at[rows - tile : rows, :], ends_ref.at[1], sems.at[1]),
    ]
    for copy in copies:
        copy.start()
    for copy in copies:
        copy.wait()
    first, last = ends_ref[0, 0:reach, :], ends_ref[1, tile - reach :, :]
    even = lax.rem(lax.axis_index("seq"), 2) == 0
    near_ref[...] = jnp.where(even, last, first)
    far_ref[...] = jnp.where(even, first, last)


def norm_kernel(x_ref, gain_ref, normed_ref):
    normed_ref[...] = normed_rows(x_ref[...], gain_ref[...]).astype(BF16)


def center_kernel(reach, normed_ref, near_ref, gain_ref, w_ref, part_ref, *shift_refs):
    rows, chan = normed_ref.shape
    taps, _, out_chan = w_ref.shape
    total = dot(normed_ref[...], w_ref[(taps - 1) // 2])
    even = lax.rem(lax.axis_index("seq"), 2) == 0
    near = normed_rows(near_ref[...], gain_ref[...])
    spare = jnp.zeros((16 * pl.cdiv(reach, 16) - reach, chan), F32)
    line = jnp.concatenate([normed_ref[...], jnp.concatenate([near, spare], axis=0).astype(BF16)], axis=0)
    blank = jnp.zeros((reach, out_chan), F32)
    slots = iter(shift_refs)
    for tap in range(taps):
        shift = (tap - (taps - 1) // 2) * DILATION_STEP
        if shift == 0:
            continue
        shift_ref = next(slots)
        product = dot(line, w_ref[tap])
        beside = product[rows : rows + reach]
        if shift < 0:
            shift_ref[0 : 2 * reach, :] = jnp.concatenate([blank, jnp.where(even, 0.0, beside)], axis=0)
            shift_ref[2 * reach :, :] = product[0:rows]
            total = total + shift_ref[2 * reach + shift : 2 * reach + shift + rows, :]
        else:
            shift_ref[0:rows, :] = product[0:rows]
            shift_ref[rows:, :] = jnp.concatenate([jnp.where(even, beside, 0.0), blank], axis=0)
            total = total + shift_ref[shift : shift + rows, :]
    part_ref[...] = total


def project_kernel(
    reach, x_ref, part_ref, far_ref, gain_ref, w_ref, bias_ref, again_ref, wk_ref, wv_ref,
    hidden_ref, attn_ref, kv_ref, keys_ref,
):
    rows, chan = x_ref.shape
    taps, _, out_chan = w_ref.shape
    index, count = lax.axis_index("seq"), lax.axis_size("seq")
    even = lax.rem(index, 2) == 0
    outside = (index == 0) | (index == count - 1)
    far = far_ref[...].astype(F32)
    factor = jnp.where(outside, 0.0, lax.rsqrt(jnp.mean(far * far, axis=-1, keepdims=True) + EPS))
    far = far * gain_ref[...]
    edge = 16 * pl.cdiv(reach, 16)
    far = jnp.concatenate([far, jnp.zeros((edge - reach, chan), F32)], axis=0).astype(BF16)
    top, bottom = part_ref[0:edge, :], part_ref[rows - edge :, :]
    middle = (taps - 1) // 2
    for away in range(1, middle + 1):
        shift = away * DILATION_STEP
        extra = dot(far, w_ref[jnp.where(even, middle - away, middle + away)])[0:reach] * factor
        blank = jnp.zeros((edge - shift, out_chan), F32)
        top = top + jnp.where(even, jnp.concatenate([extra[reach - shift : reach], blank], axis=0), 0.0)
        bottom = bottom + jnp.where(even, 0.0, jnp.concatenate([blank, extra[0:shift]], axis=0))

    def activate(span, total):
        activated = jax.nn.gelu(total + bias_ref[...], approximate=True)
        first = (x_ref[span, :out_chan].astype(F32) + activated).astype(BF16)
        hidden = jnp.concatenate([first, x_ref[span, out_chan:]], axis=1)
        hidden_ref[span, :] = hidden
        attn_ref[span, :] = normed_rows(hidden, again_ref[...]).astype(BF16)

    both = jnp.concatenate([wk_ref[...], wv_ref[...]], axis=1)
    head_dim = wk_ref.shape[1]

    def keep(span, pair):
        keys_ref[span, :] = pair[:, :head_dim]
        square = span.start // head_dim
        at = span.start - square * head_dim
        kv_ref[head_dim + at : head_dim + at + pair.shape[0], square * head_dim : (square + 1) * head_dim] = pair[:, head_dim:]

    cuts = [edge] + list(range(head_dim, rows, head_dim)) + [rows - edge]
    for span in [slice(*pair) for pair in zip(cuts, cuts[1:])]:
        activate(span, part_ref[span, :])
        keep(span, dot(attn_ref[span, :], both).astype(BF16))
    activate(slice(0, edge), top)
    activate(slice(rows - edge, rows), bottom)
    ends = jnp.concatenate([attn_ref[0:edge, :], attn_ref[rows - edge :, :]], axis=0)
    ends = dot(ends, both).astype(BF16)
    keep(slice(0, edge), ends[:edge])
    keep(slice(rows - edge, rows), ends[edge:])
    kv_ref[0:head_dim, :] = keys_ref[...].T


def key_side(kv, head_dim):
    ones = (lax.broadcasted_iota(jnp.int32, (head_dim, kv.shape[1]), 0) == 0).astype(BF16)
    return jnp.concatenate([kv[0:head_dim, :], ones], axis=0)


def value_side(kv, head_dim):
    rows = kv.shape[1]
    values = [kv[head_dim:, at : at + head_dim] for at in range(0, rows, head_dim)]
    return jnp.concatenate([jnp.concatenate(values, axis=0), jnp.ones((rows, head_dim), BF16)], axis=1)


def fold(q_ref, kv_refs, acc_in, acc_out):
    many, head_dim = q_ref.shape[0], q_ref.shape[1] // 2
    scale = LOG2E * head_dim**-0.5
    step = math.gcd(many, 256)
    pairs = [(key_side(kv, head_dim), value_side(kv, head_dim)) for kv in kv_refs]
    for at in range(0, many, step):
        span = slice(at, at + step)
        total = acc_in[span, :]
        for keys, values in pairs:
            scores = dot(q_ref[span, :], keys) * scale
            weights = jnp.exp2(jnp.minimum(scores, CEILING))
            total = total + dot(weights.astype(BF16), values)
        acc_out[span, :] = total


def exact(q_ref, kv_refs, acc_out):
    many, head_dim = q_ref.shape[0], q_ref.shape[1] // 2
    scale = LOG2E * head_dim**-0.5
    step = math.gcd(many, 256)
    pairs = [(kv[0:head_dim, :], value_side(kv, head_dim)) for kv in kv_refs]
    for at in range(0, many, step):
        span = slice(at, at + step)
        scores = [dot(q_ref[span, :head_dim], keys) * scale for keys, _ in pairs]
        top = jnp.max(functools.reduce(jnp.maximum, scores), axis=-1, keepdims=True)
        total = None
        for s, (_, values) in zip(scores, pairs):
            piece = dot(jnp.exp2(s - top).astype(BF16), values)
            total = piece if total is None else total + piece
        acc_out[span, :] = total


def query_kernel(attn_ref, wq_ref, kv_ref, q_ref, acc_ref):
    rows = attn_ref.shape[0]
    head_dim = q_ref.shape[1] // 2
    scale = LOG2E * head_dim**-0.5
    q = dot(attn_ref[...], wq_ref[...])
    keys, values = kv_ref[0:head_dim, :], value_side(kv_ref, head_dim)
    for h in range(wq_ref.shape[1] // head_dim):
        span = slice(h * rows, (h + 1) * rows)
        q_head = q[:, h * head_dim : (h + 1) * head_dim].astype(BF16)
        scores = dot(q_head, keys)
        top = jnp.broadcast_to(jnp.max(scores, axis=-1, keepdims=True), (rows, head_dim)).astype(BF16)
        q_ref[span, :head_dim] = q_head
        q_ref[span, head_dim:] = -top
        top = jnp.concatenate([top.astype(F32)] * (scores.shape[1] // head_dim), axis=1)
        acc_ref[span, :] = dot(jnp.exp2((scores - top) * scale).astype(BF16), values)


def more_kernel(q_ref, acc_in, *rest):
    fold(q_ref, rest[:-1], acc_in, rest[-1])


def last_kernel(blocks, q_ref, acc_in, hidden_ref, wo_ref, *rest):
    kv_refs = rest[:blocks]
    out_hbm, acc_ref, out_ref, sems = rest[-4:]
    rows, chan = hidden_ref.shape
    many, head_dim = q_ref.shape[0], q_ref.shape[1] // 2
    width = chan // sems.shape[0]

    def finish():
        attended = jnp.concatenate(
            [
                (acc_ref[at : at + rows, :head_dim] / acc_ref[at : at + rows, head_dim:]).astype(BF16)
                for at in range(0, many, rows)
            ],
            axis=1,
        )
        copies = []
        for i in range(sems.shape[0]):
            span = slice(i * width, (i + 1) * width)
            out_ref[:, span] = (hidden_ref[:, span].astype(F32) + dot(attended, wo_ref[:, span])).astype(BF16)
            copies.append(pltpu.make_async_copy(out_ref.at[:, span], out_hbm.at[:, span], sems.at[i]))
            copies[-1].start()
        return copies

    fold(q_ref, kv_refs, acc_in, acc_ref)
    copies = finish()
    sums = acc_ref[:, head_dim:]
    good = (jnp.max(sums) <= 2.0**LIMIT) & (jnp.min(sums) >= 2.0**-LIMIT)
    for copy in copies:
        copy.wait()

    @pl.when(jnp.logical_not(good))
    def _():
        exact(q_ref, rest[:-4], acc_ref)
        for copy in finish():
            copy.wait()


def call(body, outs, args, specs=None, scratch=(), flops=0, moved=0, name=None, alias=None, out_spec=VMEM):
    return pl.pallas_call(
        body,
        out_shape=outs,
        in_specs=specs or [VMEM] * len(args),
        out_specs=jax.tree.map(lambda _: out_spec, outs),
        scratch_shapes=scratch,
        input_output_aliases=alias or {},
        compiler_params=pltpu.CompilerParams(vmem_limit_bytes=16 * 1024 * 1024),
        cost_estimate=pl.CostEstimate(flops=flops, bytes_accessed=moved, transcendentals=0),
        name=name,
    )(*args)


def shards(
    seq_in, conv_gain, convolution_weight, conv_bias, attn_gain, w_query, w_key, w_value, w_out
):
    rows, chan = seq_in.shape
    taps, _, out_chan = convolution_weight.shape
    head_dim = w_key.shape[1]
    heads = w_query.shape[1] // head_dim
    reach = DILATION_STEP * (taps - 1) // 2
    count = lax.axis_size("seq")
    shape = jax.ShapeDtypeStruct

    near, far = call(
        functools.partial(edge_kernel, reach),
        (shape((reach, chan), BF16),) * 2,
        (pltpu.with_memory_space_constraint(seq_in, pltpu.HBM),),
        specs=[pl.BlockSpec(memory_space=pltpu.HBM)],
        scratch=[pltpu.VMEM((2, 16 * pl.cdiv(reach, 16), chan), BF16), pltpu.SemaphoreType.DMA((2,))],
        flops=LOADF,
        moved=rows * chan * 4,
        name="edges",
    )
    far_pairs = [(i, (i - 1 if i % 2 == 0 else i + 1) % count) for i in range(count)]
    far = lax.ppermute(far, "seq", far_pairs)
    near = lax.ppermute(near, "seq", [(i, i ^ 1) for i in range(count)])
    normed = call(norm_kernel, shape((rows, chan), BF16), (seq_in, conv_gain), flops=4 * rows * chan, name="norm")
    part = call(
        functools.partial(center_kernel, reach),
        shape((rows, out_chan), F32),
        (normed, near, conv_gain, convolution_weight),
        scratch=[pltpu.VMEM((rows + 2 * reach, out_chan), F32)] * (taps - 1),
        flops=2 * rows * chan * out_chan * taps,
        moved=rows * chan * 4 + chan * out_chan * 2,
        name="center",
    )
    hidden, attn_in, kv = call(
        functools.partial(project_kernel, reach),
        (shape((rows, chan), BF16), shape((rows, chan), BF16), shape((2 * head_dim, rows), BF16)),
        (seq_in, part, far, conv_gain, convolution_weight, conv_bias, attn_gain, w_key, w_value),
        scratch=[pltpu.VMEM((rows, head_dim), BF16)],
        flops=2 * rows * chan * 2 * head_dim,
        name="project",
    )
    steps = list(range(2, count, 2))
    blocks = []
    for k, step in enumerate(steps):
        other = steps[k ^ 1] if (k ^ 1) < len(steps) else step
        blocks.append(lax.ppermute(kv, "seq", [(i, i ^ (step, other)[i % 2]) for i in range(count)]))
    sibling = [(i, i ^ 1) for i in range(count)]
    mate = lax.ppermute(kv, "seq", sibling)
    fold_flops = 4 * rows * rows * heads * head_dim
    q_shape, acc_shape = shape((rows * heads, 2 * head_dim), BF16), shape((rows * heads, 2 * head_dim), F32)
    q, acc = call(
        query_kernel,
        (q_shape, acc_shape),
        (attn_in, w_query, kv),
        flops=2 * rows * chan * heads * head_dim + fold_flops,
        name="query",
    )
    passed = []
    for k, block in enumerate(blocks):
        acc, block = lax.optimization_barrier((acc, block))
        blocks[k] = block
        passed.append(lax.ppermute(block, "seq", sibling))
        group = [block]
        if k == len(blocks) - 1:
            group = [mate, block, *passed[:-1]]
        acc = call(
            more_kernel,
            acc_shape,
            (q, acc, *group),
            alias={1: 0},
            flops=len(group) * fold_flops,
            name=f"fold{k}",
        )
    return call(
        functools.partial(last_kernel, 1),
        shape((rows, chan), BF16),
        (q, acc, hidden, w_out, passed[-1], *passed[:-1], kv, mate, *blocks),
        out_spec=pl.BlockSpec(memory_space=pltpu.HBM),
        scratch=[
            pltpu.VMEM(acc_shape.shape, F32),
            pltpu.VMEM((rows, chan), BF16),
            pltpu.SemaphoreType.DMA((3,)),
        ],
        flops=fold_flops + 2 * rows * chan * heads * head_dim,
        name="last",
    )


def solution(mesh):
    placed = (P(("dp", "seq"), None), P(), P(), P(), P(), P(), P(), P(), P())
    return jax.shard_map(
        shards, mesh=mesh, in_specs=placed, out_specs=P(("dp", "seq"), None), check_vma=False
    )
```

```python
import functools
import math

import jax
import jax.numpy as jnp
from jax import lax
from jax.experimental import pallas as pl
from jax.experimental.pallas import tpu as pltpu
from jax.sharding import PartitionSpec as P

DILATION_STEP = 4
EPS = 1e-06
CEILING = 100.0
LIMIT = 60
LOADF = 8_000_000_000
LOG2E = 1.4426950408889634
F32 = jnp.float32
BF16 = jnp.bfloat16
VMEM = pl.BlockSpec(memory_space=pltpu.VMEM)
SMEM = pl.BlockSpec(memory_space=pltpu.SMEM)


def normed_rows(values, gain):
    wide = values.astype(F32)
    meansq = jnp.mean(wide * wide, axis=-1, keepdims=True)
    return wide * lax.rsqrt(meansq + EPS) * gain


def dot(a, b):
    return jnp.dot(a, b, preferred_element_type=F32)


def edge_kernel(reach, x_hbm, near_ref, far_ref, ends_ref, sems):
    rows = x_hbm.shape[0]
    tile = ends_ref.shape[1]
    copies = [
        pltpu.make_async_copy(x_hbm.at[0:tile, :], ends_ref.at[0], sems.at[0]),
        pltpu.make_async_copy(x_hbm.at[rows - tile : rows, :], ends_ref.at[1], sems.at[1]),
    ]
    for copy in copies:
        copy.start()
    for copy in copies:
        copy.wait()
    first, last = ends_ref[0, 0:reach, :], ends_ref[1, tile - reach :, :]
    even = lax.rem(lax.axis_index("seq"), 2) == 0
    near_ref[...] = jnp.where(even, last, first)
    far_ref[...] = jnp.where(even, first, last)


def norm_kernel(x_ref, gain_ref, normed_ref):
    normed_ref[...] = normed_rows(x_ref[...], gain_ref[...]).astype(BF16)


def center_kernel(reach, normed_ref, near_ref, gain_ref, w_ref, part_ref, *shift_refs):
    rows, chan = normed_ref.shape
    taps, _, out_chan = w_ref.shape
    total = dot(normed_ref[...], w_ref[(taps - 1) // 2])
    even = lax.rem(lax.axis_index("seq"), 2) == 0
    near = normed_rows(near_ref[...], gain_ref[...])
    spare = jnp.zeros((16 * pl.cdiv(reach, 16) - reach, chan), F32)
    line = jnp.concatenate([normed_ref[...], jnp.concatenate([near, spare], axis=0).astype(BF16)], axis=0)
    blank = jnp.zeros((reach, out_chan), F32)
    slots = iter(shift_refs)
    for tap in range(taps):
        shift = (tap - (taps - 1) // 2) * DILATION_STEP
        if shift == 0:
            continue
        shift_ref = next(slots)
        product = dot(line, w_ref[tap])
        beside = product[rows : rows + reach]
        if shift < 0:
            shift_ref[0 : 2 * reach, :] = jnp.concatenate([blank, jnp.where(even, 0.0, beside)], axis=0)
            shift_ref[2 * reach :, :] = product[0:rows]
            total = total + shift_ref[2 * reach + shift : 2 * reach + shift + rows, :]
        else:
            shift_ref[0:rows, :] = product[0:rows]
            shift_ref[rows:, :] = jnp.concatenate([jnp.where(even, beside, 0.0), blank], axis=0)
            total = total + shift_ref[shift : shift + rows, :]
    part_ref[...] = total


def project_kernel(
    reach, x_ref, part_ref, far_ref, gain_ref, w_ref, bias_ref, again_ref, wk_ref, wv_ref,
    hidden_ref, attn_ref, kv_ref, keys_ref,
):
    rows, chan = x_ref.shape
    taps, _, out_chan = w_ref.shape
    index, count = lax.axis_index("seq"), lax.axis_size("seq")
    even = lax.rem(index, 2) == 0
    outside = (index == 0) | (index == count - 1)
    far = far_ref[...].astype(F32)
    factor = jnp.where(outside, 0.0, lax.rsqrt(jnp.mean(far * far, axis=-1, keepdims=True) + EPS))
    far = far * gain_ref[...]
    edge = 16 * pl.cdiv(reach, 16)
    far = jnp.concatenate([far, jnp.zeros((edge - reach, chan), F32)], axis=0).astype(BF16)
    top, bottom = part_ref[0:edge, :], part_ref[rows - edge :, :]
    middle = (taps - 1) // 2
    for away in range(1, middle + 1):
        shift = away * DILATION_STEP
        extra = dot(far, w_ref[jnp.where(even, middle - away, middle + away)])[0:reach] * factor
        blank = jnp.zeros((edge - shift, out_chan), F32)
        top = top + jnp.where(even, jnp.concatenate([extra[reach - shift : reach], blank], axis=0), 0.0)
        bottom = bottom + jnp.where(even, 0.0, jnp.concatenate([blank, extra[0:shift]], axis=0))

    def activate(span, total):
        activated = jax.nn.gelu(total + bias_ref[...], approximate=True)
        first = (x_ref[span, :out_chan].astype(F32) + activated).astype(BF16)
        hidden = jnp.concatenate([first, x_ref[span, out_chan:]], axis=1)
        hidden_ref[span, :] = hidden
        attn_ref[span, :] = normed_rows(hidden, again_ref[...]).astype(BF16)

    both = jnp.concatenate([wk_ref[...], wv_ref[...]], axis=1)
    head_dim = wk_ref.shape[1]

    def keep(span, pair):
        keys_ref[span, :] = pair[:, :head_dim]
        square = span.start // head_dim
        at = span.start - square * head_dim
        kv_ref[head_dim + at : head_dim + at + pair.shape[0], square * head_dim : (square + 1) * head_dim] = pair[:, head_dim:]

    cuts = [edge] + list(range(head_dim, rows, head_dim)) + [rows - edge]
    for span in [slice(*pair) for pair in zip(cuts, cuts[1:])]:
        activate(span, part_ref[span, :])
        keep(span, dot(attn_ref[span, :], both).astype(BF16))
    activate(slice(0, edge), top)
    activate(slice(rows - edge, rows), bottom)
    ends = jnp.concatenate([attn_ref[0:edge, :], attn_ref[rows - edge :, :]], axis=0)
    ends = dot(ends, both).astype(BF16)
    keep(slice(0, edge), ends[:edge])
    keep(slice(rows - edge, rows), ends[edge:])
    kv_ref[0:head_dim, :] = keys_ref[...].T


def key_side(kv, head_dim):
    ones = (lax.broadcasted_iota(jnp.int32, (head_dim, kv.shape[1]), 0) == 0).astype(BF16)
    return jnp.concatenate([kv[0:head_dim, :], ones], axis=0)


def value_side(kv, head_dim):
    rows = kv.shape[1]
    values = [kv[head_dim:, at : at + head_dim] for at in range(0, rows, head_dim)]
    return jnp.concatenate([jnp.concatenate(values, axis=0), jnp.ones((rows, head_dim), BF16)], axis=1)


def fold(q_ref, kv_refs, acc_in, acc_out):
    many, head_dim = q_ref.shape[0], q_ref.shape[1] // 2
    scale = LOG2E * head_dim**-0.5
    step = math.gcd(many, 256)
    pairs = [(key_side(kv, head_dim), value_side(kv, head_dim)) for kv in kv_refs]
    for at in range(0, many, step):
        span = slice(at, at + step)
        total = acc_in[span, :]
        for keys, values in pairs:
            scores = dot(q_ref[span, :], keys) * scale
            weights = jnp.exp2(jnp.minimum(scores, CEILING))
            total = total + dot(weights.astype(BF16), values)
        acc_out[span, :] = total


def exact(q_ref, kv_refs, acc_out):
    many, head_dim = q_ref.shape[0], q_ref.shape[1] // 2
    scale = LOG2E * head_dim**-0.5
    step = math.gcd(many, 256)
    pairs = [(kv[0:head_dim, :], value_side(kv, head_dim)) for kv in kv_refs]
    for at in range(0, many, step):
        span = slice(at, at + step)
        scores = [dot(q_ref[span, :head_dim], keys) * scale for keys, _ in pairs]
        top = jnp.max(functools.reduce(jnp.maximum, scores), axis=-1, keepdims=True)
        total = None
        for s, (_, values) in zip(scores, pairs):
            piece = dot(jnp.exp2(s - top).astype(BF16), values)
            total = piece if total is None else total + piece
        acc_out[span, :] = total


def query_kernel(attn_ref, wq_ref, kv_ref, q_ref, acc_ref):
    rows = attn_ref.shape[0]
    head_dim = q_ref.shape[1] // 2
    scale = LOG2E * head_dim**-0.5
    q = dot(attn_ref[...], wq_ref[...])
    keys, values = kv_ref[0:head_dim, :], value_side(kv_ref, head_dim)
    for h in range(wq_ref.shape[1] // head_dim):
        span = slice(h * rows, (h + 1) * rows)
        q_head = q[:, h * head_dim : (h + 1) * head_dim].astype(BF16)
        scores = dot(q_head, keys)
        top = jnp.broadcast_to(jnp.max(scores, axis=-1, keepdims=True), (rows, head_dim)).astype(BF16)
        q_ref[span, :head_dim] = q_head
        q_ref[span, head_dim:] = -top
        top = jnp.concatenate([top.astype(F32)] * (scores.shape[1] // head_dim), axis=1)
        acc_ref[span, :] = dot(jnp.exp2((scores - top) * scale).astype(BF16), values)


def more_kernel(q_ref, acc_in, *rest):
    fold(q_ref, rest[:-1], acc_in, rest[-1])


def last_kernel(blocks, q_ref, acc_in, hidden_ref, wo_ref, *rest):
    kv_refs = rest[:blocks]
    out_hbm, acc_ref, out_ref, sems = rest[-4:]
    rows, chan = hidden_ref.shape
    many, head_dim = q_ref.shape[0], q_ref.shape[1] // 2
    width = chan // sems.shape[0]

    def finish():
        attended = jnp.concatenate(
            [
                (acc_ref[at : at + rows, :head_dim] / acc_ref[at : at + rows, head_dim:]).astype(BF16)
                for at in range(0, many, rows)
            ],
            axis=1,
        )
        copies = []
        for i in range(sems.shape[0]):
            span = slice(i * width, (i + 1) * width)
            out_ref[:, span] = (hidden_ref[:, span].astype(F32) + dot(attended, wo_ref[:, span])).astype(BF16)
            copies.append(pltpu.make_async_copy(out_ref.at[:, span], out_hbm.at[:, span], sems.at[i]))
            copies[-1].start()
        return copies

    fold(q_ref, kv_refs, acc_in, acc_ref)
    copies = finish()
    sums = acc_ref[:, head_dim:]
    good = (jnp.max(sums) <= 2.0**LIMIT) & (jnp.min(sums) >= 2.0**-LIMIT)
    for copy in copies:
        copy.wait()

    @pl.when(jnp.logical_not(good))
    def _():
        exact(q_ref, rest[:-4], acc_ref)
        for copy in finish():
            copy.wait()


def call(body, outs, args, specs=None, scratch=(), flops=0, moved=0, name=None, alias=None, out_spec=VMEM):
    return pl.pallas_call(
        body,
        out_shape=outs,
        in_specs=specs or [VMEM] * len(args),
        out_specs=jax.tree.map(lambda _: out_spec, outs),
        scratch_shapes=scratch,
        input_output_aliases=alias or {},
        compiler_params=pltpu.CompilerParams(vmem_limit_bytes=16 * 1024 * 1024),
        cost_estimate=pl.CostEstimate(flops=flops, bytes_accessed=moved, transcendentals=0),
        name=name,
    )(*args)


def shards(
    seq_in, conv_gain, convolution_weight, conv_bias, attn_gain, w_query, w_key, w_value, w_out
):
    rows, chan = seq_in.shape
    taps, _, out_chan = convolution_weight.shape
    head_dim = w_key.shape[1]
    heads = w_query.shape[1] // head_dim
    reach = DILATION_STEP * (taps - 1) // 2
    count = lax.axis_size("seq")
    shape = jax.ShapeDtypeStruct

    near, far = call(
        functools.partial(edge_kernel, reach),
        (shape((reach, chan), BF16),) * 2,
        (pltpu.with_memory_space_constraint(seq_in, pltpu.HBM),),
        specs=[pl.BlockSpec(memory_space=pltpu.HBM)],
        scratch=[pltpu.VMEM((2, 16 * pl.cdiv(reach, 16), chan), BF16), pltpu.SemaphoreType.DMA((2,))],
        flops=LOADF,
        moved=rows * chan * 4,
        name="edges",
    )
    far_pairs = [(i, (i - 1 if i % 2 == 0 else i + 1) % count) for i in range(count)]
    far = lax.ppermute(far, "seq", far_pairs)
    near = lax.ppermute(near, "seq", [(i, i ^ 1) for i in range(count)])
    normed = call(norm_kernel, shape((rows, chan), BF16), (seq_in, conv_gain), flops=4 * rows * chan, name="norm")
    part = call(
        functools.partial(center_kernel, reach),
        shape((rows, out_chan), F32),
        (normed, near, conv_gain, convolution_weight),
        scratch=[pltpu.VMEM((rows + 2 * reach, out_chan), F32)] * (taps - 1),
        flops=2 * rows * chan * out_chan * taps,
        moved=rows * chan * 4 + chan * out_chan * 2,
        name="center",
    )
    hidden, attn_in, kv = call(
        functools.partial(project_kernel, reach),
        (shape((rows, chan), BF16), shape((rows, chan), BF16), shape((2 * head_dim, rows), BF16)),
        (seq_in, part, far, conv_gain, convolution_weight, conv_bias, attn_gain, w_key, w_value),
        scratch=[pltpu.VMEM((rows, head_dim), BF16)],
        flops=2 * rows * chan * 2 * head_dim,
        name="project",
    )
    chips = count // 2
    ring = [place ^ (place >> 1) for place in range(chips)]
    rounds = []
    for turn in range(1, (chips + 1) // 2):
        rounds += [(turn, chips - turn), (chips - turn, turn)]
    if chips % 2 == 0:
        rounds.append((chips // 2, chips // 2))
    rounds = [(y, x) for x, y in rounds]
    blocks = []
    for turns in rounds:
        moves = [(place, core) for place in range(chips) for core in range(2)]
        blocks.append(
            lax.ppermute(
                kv,
                "seq",
                [(2 * ring[p] + core, 2 * ring[(p + turns[core]) % chips] + core) for p, core in moves],
            )
        )
    sibling = [(i, i ^ 1) for i in range(count)]
    mate = lax.ppermute(kv, "seq", sibling)
    fold_flops = 4 * rows * rows * heads * head_dim
    q_shape, acc_shape = shape((rows * heads, 2 * head_dim), BF16), shape((rows * heads, 2 * head_dim), F32)
    q, acc = call(
        query_kernel,
        (q_shape, acc_shape),
        (attn_in, w_query, kv),
        flops=2 * rows * chan * heads * head_dim + fold_flops,
        name="query",
    )
    passed = []
    for k, block in enumerate(blocks):
        acc, block = lax.optimization_barrier((acc, block))
        blocks[k] = block
        passed.append(lax.ppermute(block, "seq", sibling))
        group = [block]
        if k == len(blocks) - 1:
            group = [mate, block, *passed[:-1]]
        acc = call(
            more_kernel,
            acc_shape,
            (q, acc, *group),
            alias={1: 0},
            flops=len(group) * fold_flops,
            name=f"fold{k}",
        )
    return call(
        functools.partial(last_kernel, 1),
        shape((rows, chan), BF16),
        (q, acc, hidden, w_out, passed[-1], *passed[:-1], kv, mate, *blocks),
        out_spec=pl.BlockSpec(memory_space=pltpu.HBM),
        scratch=[
            pltpu.VMEM(acc_shape.shape, F32),
            pltpu.VMEM((rows, chan), BF16),
            pltpu.SemaphoreType.DMA((3,)),
        ],
        flops=fold_flops + 2 * rows * chan * heads * head_dim,
        name="last",
    )


def solution(mesh):
    placed = (P(("dp", "seq"), None), P(), P(), P(), P(), P(), P(), P(), P())
    return jax.shard_map(
        shards, mesh=mesh, in_specs=placed, out_specs=P(("dp", "seq"), None), check_vma=False
    )
```
